256 devices in a mesh: grp: 4 (over z_lo, core), dev: 64 (over y, z_hi, x).
Axes of the slice: x: 4, y: 4, z: 8 (z_hi: 4, z_lo: 2; z = z_hi * 2 + z_lo), core: 2. Of those that a mesh axis runs over, the one named last changes fastest.
Arguments:
- field: bfloat16 [1024, 222, 4096], P(('grp', 'dev')), may hold values from -6 to 6
- level_start: float32 [222, 48], replicated, may hold values from -0.375 to 0.375
- time_start: float32 [768, 128], replicated, may hold values from -0.21875 to 0.21875
- lag_offsets: int32 [8], replicated, may hold values from 0 to 256, as said below
Outputs:
- level_basis: float32 [222, 48], replicated
- low_rank: float32 [768, 768], replicated
The draws below stay inside these ranges and needn't reach their ends.
Inputs may be any that keep to these rules, and one draw needn't show every extreme that they name: `lag_offsets`: the first offset is 0 and the last is 256; offsets are distinct.
All inputs are finite; a program needn't handle non-finite values.
Results may differ from the reference program's by a relative error of at most 0.0014.
The reference program's roundings to bfloat16 on the way (of `basis_low` and `modes`) count: a program that leaves them out, or rounds other values in their place, can miss the bound.
Values may be sent and summed in bfloat16 or wider, within the bound.
No kernel may reach another device: no remote copies, remote signals or barrier semaphores. Data moves between devices by JAX's collectives and lax.ppermute only.
A program may use at most 128 MiB of HBM per device.

```python
import jax
import jax.numpy as jnp
from jax import lax

F = 222
MODES = 48
NLAG = 8
ITERS = 3
COLS = 4096
TOTAL = 1024
MAXLAG = 256
W = 768
RANK = 128


def draw_lag_offsets(key, part):
    key = jax.random.fold_in(key, 7)
    middle = jax.random.permutation(key, MAXLAG - 1)[:NLAG - 2] + 1
    middle = jnp.sort(middle)
    first = jnp.zeros((1,), jnp.int32)
    last = jnp.full((1,), MAXLAG, jnp.int32)
    return jnp.concatenate([first, middle.astype(jnp.int32), last]).astype(jnp.int32)


def block_levels(key, extent, pieces, least, high):
    level = 1.0
    for dim, parts in pieces:
        draws = jax.random.uniform(jax.random.fold_in(jax.random.fold_in(key, 6), dim), (parts,), jnp.float32, least / len(pieces), high / len(pieces))
        level = level * jnp.repeat(jnp.exp(draws), extent[dim] // parts).reshape((-1,) + (1,) * (len(extent) - 1 - dim))
    return level


def noise(key, extent, scale, reach, cuts=(), held_as=jnp.bfloat16):
    loudness = block_levels(key, extent, cuts, -0.22, 0.18) if cuts else 1.0
    array = jax.random.normal(key, extent, jnp.float32) * scale * loudness
    return jnp.minimum(jnp.maximum(array, -reach), reach).astype(held_as)


def setup_inputs(seed: int = 0) -> dict:
    seeds = jax.random.split(jax.random.key(seed), 5)
    field = noise(seeds[0], (TOTAL, F, COLS), 1.0, 6.0, ((0, 256),))
    level_start = noise(seeds[1], (F, MODES), F ** -0.5, 0.375, (), jnp.float32)
    time_start = noise(seeds[2], (W, RANK), W ** -0.5, 0.21875, (), jnp.float32)
    lag_offsets = draw_lag_offsets(jax.random.fold_in(seeds[4], 71), 0)
    return dict(field=field, level_start=level_start, time_start=time_start, lag_offsets=lag_offsets)


HIGH = lax.Precision.HIGHEST

def orth(z):
    low = jnp.linalg.cholesky(jnp.dot(z.T, z, precision=HIGH))
    return lax.linalg.triangular_solve(low, z, left_side=False, lower=True, transpose_a=True)

def lag_sum(gram, offsets, width):

    def step(j, acc):
        start = offsets[j].astype(jnp.int32)
        return acc + lax.dynamic_slice(gram, (start, start), (width, width))
    return lax.fori_loop(0, offsets.shape[0], step, jnp.zeros((width, width), jnp.float32))

def debias(lagged):
    rows = jnp.mean(lagged, axis=1)
    return lagged - rows[:, None] - rows[None, :] + jnp.mean(lagged)

def truncate(debiased, start):
    basis = start
    for step in range(ITERS):
        basis = orth(jnp.dot(debiased, basis, precision=HIGH))
    inner = jnp.dot(basis.T, jnp.dot(debiased, basis, precision=HIGH), precision=HIGH)
    return jnp.dot(jnp.dot(basis, inner, precision=HIGH), basis.T, precision=HIGH)

def reference(field, level_start, time_start, lag_offsets):

    def add_hour(acc, hour):
        return (acc + jnp.dot(hour.astype(jnp.float32), hour.T.astype(jnp.float32), preferred_element_type=jnp.float32), None)
    level_gram, unused = lax.scan(add_hour, jnp.zeros((F, F), jnp.float32), field)
    level_gram = level_gram / (TOTAL * COLS)
    level_basis = orth(jnp.dot(level_gram, level_start, precision=HIGH))
    basis_low = level_basis.astype(jnp.bfloat16)

    def project(hour):
        return jnp.dot(basis_low.T.astype(jnp.float32), hour.astype(jnp.float32), preferred_element_type=jnp.float32).astype(jnp.bfloat16)
    modes = lax.map(project, field)
    flat = modes.reshape(TOTAL, MODES * COLS)
    hour_gram = jnp.dot(flat.astype(jnp.float32), flat.T.astype(jnp.float32), preferred_element_type=jnp.float32)
    lagged = lag_sum(hour_gram, lag_offsets, W) / (NLAG * MODES * COLS)
    low_rank = truncate(debias(lagged), time_start)
    return (level_basis, low_rank)
```

```python
import jax
import jax.numpy as jnp
from jax import lax
from jax.sharding import Mesh, PartitionSpec as P

ITERS = 3
AXES = ("zl", "co", "y", "zh", "x")
SIZES = (2, 2, 4, 4, 4)

HIGH = lax.Precision.HIGHEST


def orth(z):
    low = jnp.linalg.cholesky(jnp.dot(z.T, z, precision=HIGH))
    return lax.linalg.triangular_solve(low, z, left_side=False, lower=True, transpose_a=True)


def lag_sum(gram, offsets, width):
    acc = jnp.zeros((width, width), jnp.float32)
    for j in range(offsets.shape[0]):
        acc = acc + lax.dynamic_slice(gram, (offsets[j], offsets[j]), (width, width))
    return acc


def debias(lagged):
    rows = jnp.mean(lagged, axis=1)
    return lagged - rows[:, None] - rows[None, :] + jnp.mean(lagged)


def truncate(debiased, start):
    basis = start
    for step in range(ITERS):
        basis = orth(jnp.dot(debiased, basis, precision=HIGH))
    inner = jnp.dot(basis.T, jnp.dot(debiased, basis, precision=HIGH), precision=HIGH)
    return jnp.dot(jnp.dot(basis, inner, precision=HIGH), basis.T, precision=HIGH)


def swap(x, axis, k):
    n = SIZES[AXES.index(axis)] if isinstance(axis, str) else 4
    return lax.ppermute(x, axis, [(i, i ^ k) for i in range(n)])


def all_sum(x, axis):
    got = [swap(x, axis, k) for k in (1, 2, 3)]
    return (x + got[0]) + (got[1] + got[2])


def scatter_sum(x, axis):
    n = x.shape[0]
    got = [swap(x[k], axis, k) for k in range(1, n)]
    if n == 2:
        return x[0] + got[0]
    return (x[0] + got[0]) + (got[1] + got[2])


def gather(x, axis, n):
    return jnp.stack([x] + [swap(x, axis, k) for k in range(1, n)])


def sum_pieces(pieces):
    x = pieces.reshape((2, 4, 4) + pieces.shape[1:])
    x = scatter_sum(x, "co")
    x = scatter_sum(x, "x")
    x = scatter_sum(x, "y")
    x = x + swap(x, "zl", 1)
    x = all_sum(x, "zh")
    x = gather(x, "y", 4)
    x = gather(x, "x", 4)
    x = gather(x, "co", 2)
    return x.reshape(pieces.shape)


def body(field, level_start, time_start, lag_offsets):
    hour_count, levels, columns = field.shape
    devices = lax.axis_size(AXES)
    hours_all = hour_count * devices
    width = time_start.shape[0]
    nmodes = level_start.shape[1]
    local_gram = jnp.einsum("hfc,hgc->fg", field, field, preferred_element_type=jnp.float32)
    local_gram = local_gram / (hours_all * columns)
    z = jnp.dot(level_start.T, local_gram, precision=HIGH)
    z = all_sum(z, ("zl", "co"))
    for axis in ("x", "y", "zh"):
        z = all_sum(z, axis)
    level_basis = orth(z.T)
    basis_low = level_basis.astype(jnp.bfloat16)
    modes = jnp.einsum("fk,hfc->hkc", basis_low, field, preferred_element_type=jnp.float32).astype(
        jnp.bfloat16
    )
    sent = modes.reshape(hour_count, 8, 6, 32, 128).transpose(1, 3, 2, 0, 4).reshape(devices, 24, 128)
    received = lax.all_to_all(sent, AXES, split_axis=0, concat_axis=0, tiled=True)
    flat = received.reshape(devices, 6, hour_count, 128).transpose(0, 2, 1, 3).reshape(hours_all, 768)
    local_hours = jnp.dot(flat, flat.T, preferred_element_type=jnp.float32)
    scale = 1.0 / (lag_offsets.shape[0] * nmodes * columns)
    lagged = lag_sum(local_hours, lag_offsets, width) * scale
    place = lax.axis_index("co") * 16 + lax.axis_index("x") * 4 + lax.axis_index("y")
    order = jnp.arange(32) ^ place
    pieces = lagged.reshape(32, width // 32, width)
    summed = sum_pieces(pieces[order])[order]
    low_rank = truncate(debias(summed.reshape(width, width)), time_start)
    return (level_basis, low_rank)


def solution(mesh):
    fine = Mesh(mesh.devices.reshape(SIZES), AXES)
    return jax.shard_map(
        body,
        mesh=fine,
        in_specs=(P(AXES, None, None), P(), P(), P()),
        out_specs=(P(), P()),
        check_vma=False,
    )
```

```python
import functools
import jax
import jax.numpy as jnp
from jax import lax
from jax.experimental import pallas as pl
from jax.experimental.pallas import tpu as pltpu
from jax.sharding import Mesh, PartitionSpec as P

AXES = ("zl", "co", "y", "zh", "x")
SIZES = (2, 2, 4, 4, 4)
HIGH = lax.Precision.HIGHEST
LANES = 128
ITERS = 3

def dot(a, b, dims=((1,), (0,)), precision=HIGH):
    return lax.dot_general(a, b, (dims, ((), ())), precision=precision, preferred_element_type=jnp.float32)


def split(x):
    hi = x.astype(jnp.bfloat16)
    rest = x - hi.astype(jnp.float32)
    mid = rest.astype(jnp.bfloat16)
    low = (rest - mid.astype(jnp.float32)).astype(jnp.bfloat16)
    return hi, mid, low


def across(row):
    return jnp.broadcast_to(row, (8, LANES))


def inverse_cholesky(gram, out_ref):
    n = gram.shape[0]
    tiles = n // 8
    lane = lax.broadcasted_iota(jnp.int32, (8, LANES), 1)
    sub = lax.broadcasted_iota(jnp.int32, (8, LANES), 0)
    left = [gram[8 * t : 8 * t + 8, :] for t in range(tiles)]
    right = [jnp.where(lane == sub + 8 * t, 1.0, 0.0) for t in range(tiles)]
    for i in range(0, n, 4):
        here, off = i // 8, i % 8
        cols = [
            {t: jnp.broadcast_to(left[t][:, i + k : i + k + 1], (8, LANES)) for t in range(here, tiles)}
            for k in range(4)
        ]
        entry = lambda r, k: across(cols[k][here][off + r : off + r + 1, :])
        low, inv = {}, []
        for k in range(4):
            for r in range(k, 4):
                v = entry(r, k)
                for q in range(k):
                    v = v - low[r, q] * low[k, q]
                if r == k:
                    inv.append(lax.rsqrt(v))
                else:
                    low[r, k] = v * inv[k]
        rows = []
        for k in range(4):
            a = across(left[here][off + k : off + k + 1, :])
            b = across(right[here][off + k : off + k + 1, :])
            for q in range(k):
                a = a - low[k, q] * rows[q][0]
                b = b - low[k, q] * rows[q][1]
            rows.append((a * inv[k], b * inv[k]))
            out_ref[i + k : i + k + 1, :] = rows[k][1][0:1, :]
        for t in range(here + (off > 0), tiles):
            mult = []
            for k in range(4):
                v = cols[k][t]
                for q in range(k):
                    v = v - mult[q] * low[k, q]
                mult.append(v * inv[k])
            for k in range(4):
                left[t] = left[t] - mult[k] * rows[k][0]
                right[t] = right[t] - mult[k] * rows[k][1]


def truncate_kernel(place_ref, pieces_ref, start_ref, out_ref, d_ref, split_ref, z_ref, w_ref, linv_ref):
    count, high, width = pieces_ref.shape
    place = place_ref[0]
    for p in range(count):
        d_ref[p * high : (p + 1) * high, :] = pieces_ref[lax.bitwise_xor(p, place)]
    lagged = d_ref[...]
    rows = jnp.sum(lagged, axis=1, keepdims=True) * (1.0 / width)
    cols = jnp.sum(lagged, axis=0, keepdims=True) * (1.0 / width)
    mean = jnp.sum(rows, axis=0, keepdims=True) * (1.0 / width)
    debiased = lagged - rows - cols + mean
    for k, part in enumerate(split(debiased)):
        split_ref[k] = part

    def times(x):
        n = x.shape[0]
        parts = jnp.concatenate(split(x), axis=0)
        by = lambda m, k: dot(parts[: m * n], split_ref[k], precision=None)
        one, two, three = by(3, 0), by(2, 1), by(1, 2)
        small = one[2 * n :] + two[n:] + three
        return one[:n] + ((one[n : 2 * n] + two[:n]) + small)

    z_ref[...] = times(start_ref[...].T)

    def step(_, carry):
        z = z_ref[...]
        inverse_cholesky(dot(z, z, ((1,), (1,))), linv_ref)
        w_ref[...] = times(z)
        @pl.when(_ < ITERS - 1)
        def _more():
            z_ref[...] = dot(linv_ref[...], w_ref[...])
        return carry

    lax.fori_loop(0, ITERS, step, 0)
    linv = linv_ref[...]
    basis = dot(linv, z_ref[...])
    inner = dot(dot(linv, w_ref[...]), basis, ((1,), (1,)))
    out_ref[...] = dot(basis, dot(inner, basis), ((0,), (0,)))


def truncate(place, pieces, start):
    width, rank = start.shape
    f32 = jnp.float32
    vm = pl.BlockSpec(memory_space=pltpu.VMEM)
    return pl.pallas_call(
        truncate_kernel,
        out_shape=jax.ShapeDtypeStruct((width, width), f32),
        in_specs=[pl.BlockSpec(memory_space=pltpu.SMEM), vm, vm],
        out_specs=vm,
        scratch_shapes=[
            pltpu.VMEM((width, width), f32),
            pltpu.VMEM((3, width, width), jnp.bfloat16),
            pltpu.VMEM((rank, width), f32),
            pltpu.VMEM((rank, width), f32),
            pltpu.VMEM((rank, rank), f32),
        ],
        compiler_params=pltpu.CompilerParams(vmem_limit_bytes=48 * 2**20),
        name="truncate",
    )(place, pieces, start)


def spread(levels, hours, turned=False):
    shape = (levels * hours, levels) if turned else (levels, levels * hours)
    place = lax.broadcasted_iota(jnp.int32, shape, 0 if turned else 1)
    level = lax.broadcasted_iota(jnp.int32, shape, 1 if turned else 0)
    return jnp.where((place >= hours * level) & (place < hours * level + hours), 1.0, 0.0).astype(jnp.bfloat16)


def level_gram_kernel(scale, field_ref, start_ref, out_ref, flat_ref, acc_ref):
    step = pl.program_id(0)
    levels, hours, chunk = field_ref.shape
    total = levels * hours
    tile = 256

    @pl.when(step == 0)
    def _():
        acc_ref[...] = jnp.zeros_like(acc_ref)

    flat = field_ref[...].reshape(total, chunk)
    flat_ref[...] = flat
    for j in range(0, total, tile):
        wide = min(tile, total - j)
        acc_ref[j:, j : j + wide] += dot(flat[j:], flat[j : j + wide], ((1,), (1,)), None)

    @pl.when(step == pl.num_programs(0) - 1)
    def _():
        row = lax.broadcasted_iota(jnp.int32, (total, total), 0)
        col = lax.broadcasted_iota(jnp.int32, (total, total), 1)
        same_hour = lax.rem(row, hours) == lax.rem(col, hours)
        same_tile = lax.div(row, tile) == lax.div(col, tile)
        half = jnp.where(same_hour, acc_ref[...] * jnp.where(same_tile, 0.5, 1.0), 0.0)
        left = spread(levels, hours)
        right = spread(levels, hours, True)
        over = sum(dot(left, part, precision=None) for part in reversed(split(half)))
        gram = sum(dot(part, right, precision=None) for part in reversed(split(over)))
        out_ref[...] = (dot(start_ref[...], gram) + dot(start_ref[...], gram, ((1,), (1,)))) * scale


def level_product(field, start, scale):
    levels, hours, columns = field.shape
    nmodes = start.shape[0]
    chunk = 1024
    return pl.pallas_call(
        functools.partial(level_gram_kernel, scale),
        grid=(columns // chunk,),
        out_shape=(
            jax.ShapeDtypeStruct((nmodes, levels), jnp.float32),
            jax.ShapeDtypeStruct((levels * hours, columns), jnp.bfloat16),
        ),
        in_specs=[
            pl.BlockSpec((levels, hours, chunk), lambda c: (0, 0, c)),
            pl.BlockSpec((nmodes, levels), lambda c: (0, 0)),
        ],
        out_specs=(
            pl.BlockSpec((nmodes, levels), lambda c: (0, 0)),
            pl.BlockSpec((levels * hours, chunk), lambda c: (0, c)),
        ),
        scratch_shapes=[pltpu.VMEM((levels * hours, levels * hours), jnp.float32)],
        compiler_params=pltpu.CompilerParams(vmem_limit_bytes=60 * 2**20),
        name="level_product",
    )(field, start)


def project_kernel(hours, z_ref, flat_ref, basis_ref, out_ref, weight_ref, linv_ref):
    total, chunk = flat_ref.shape
    nmodes, levels = z_ref.shape
    f32, bf16 = jnp.float32, jnp.bfloat16

    @pl.when(pl.program_id(0) == 0)
    def _():
        z = z_ref[...]
        gram = dot(z, z, ((1,), (1,)))
        padded = jnp.concatenate([gram, jnp.zeros((nmodes, LANES - nmodes), f32)], axis=1)
        inverse_cholesky(padded, linv_ref)
        basis = dot(linv_ref[:, :nmodes], z)
        basis_ref[...] = basis
        modes_by_hours = spread(nmodes, hours, True)
        tall = dot(modes_by_hours, basis.astype(bf16), precision=None).astype(bf16)
        wide = dot(tall, spread(levels, hours), precision=None)
        row = lax.broadcasted_iota(jnp.int32, wide.shape, 0)
        col = lax.broadcasted_iota(jnp.int32, wide.shape, 1)
        weight_ref[...] = jnp.where(lax.rem(row, hours) == lax.rem(col, hours), wide, 0.0).astype(bf16)

    made = dot(weight_ref[...], flat_ref[...], precision=None)
    groups, blocks, rows, _ = out_ref.shape
    for a in range(groups):
        for b in range(blocks):
            out_ref[a, b] = made[rows * a : rows * (a + 1), LANES * b : LANES * (b + 1)].astype(bf16)


def project(z, flat, hours, groups):
    total, columns = flat.shape
    nmodes, levels = z.shape
    chunk = 1024
    rows = hours * nmodes // groups
    return pl.pallas_call(
        functools.partial(project_kernel, hours),
        grid=(columns // chunk,),
        out_shape=(
            jax.ShapeDtypeStruct((nmodes, levels), jnp.float32),
            jax.ShapeDtypeStruct((groups, columns // LANES, rows, LANES), jnp.bfloat16),
        ),
        in_specs=[
            pl.BlockSpec((nmodes, levels), lambda c: (0, 0)),
            pl.BlockSpec((total, chunk), lambda c: (0, c)),
        ],
        out_specs=(
            pl.BlockSpec((nmodes, levels), lambda c: (0, 0)),
            pl.BlockSpec((groups, chunk // LANES, rows, LANES), lambda c: (0, c, 0, 0)),
        ),
        scratch_shapes=[
            pltpu.VMEM((hours * nmodes, total), jnp.bfloat16),
            pltpu.VMEM((nmodes, LANES), jnp.float32),
        ],
        compiler_params=pltpu.CompilerParams(vmem_limit_bytes=60 * 2**20),
        name="project",
    )(z, flat)


def lag_sum(gram, offsets, width):
    acc = jnp.zeros((width, width), jnp.float32)
    for j in range(offsets.shape[0]):
        acc = acc + lax.dynamic_slice(gram, (offsets[j], offsets[j]), (width, width))
    return acc


def swap(x, axis, k):
    n = SIZES[AXES.index(axis)] if isinstance(axis, str) else 4
    return lax.ppermute(x, axis, [(i, i ^ k) for i in range(n)])


def all_sum(x, axis):
    got = [swap(x, axis, k) for k in (1, 2, 3)]
    return (x + got[0]) + (got[1] + got[2])


def scatter_sum(x, axis):
    n = x.shape[0]
    got = [swap(x[k], axis, k) for k in range(1, n)]
    if n == 2:
        return x[0] + got[0]
    return (x[0] + got[0]) + (got[1] + got[2])


def gather(x, axis, n):
    return jnp.stack([x] + [swap(x, axis, k) for k in range(1, n)])


def sum_pieces(pieces):
    x = pieces.reshape((2, 4, 4) + pieces.shape[1:])
    x = scatter_sum(x, "co")
    x = scatter_sum(x, "x")
    x = scatter_sum(x, "y")
    x = x + swap(x, "zl", 1)
    x = all_sum(x, "zh")
    x = gather(x, "y", 4)
    x = gather(x, "x", 4)
    x = gather(x, "co", 2)
    return x.reshape(pieces.shape)


def body(field, level_start, time_start, lag_offsets):
    hour_count, levels, columns = field.shape
    devices = lax.axis_size(AXES)
    hours_all = hour_count * devices
    width = time_start.shape[0]
    nmodes = level_start.shape[1]
    scale = 1.0 / (hours_all * columns)
    z, level_hours = level_product(jnp.transpose(field, (1, 0, 2)), level_start.T, scale)
    z = all_sum(z, ("zl", "co"))
    for axis in ("x", "y", "zh"):
        z = all_sum(z, axis)
    level_basis, sent = project(z, level_hours, hour_count, 8)
    sent = sent.reshape(devices, 24, LANES)
    received = lax.all_to_all(sent, AXES, split_axis=0, concat_axis=0, tiled=True)
    flat = received.reshape(devices, 6, hour_count, LANES).transpose(0, 2, 1, 3).reshape(hours_all, 6 * LANES)
    local_hours = jnp.dot(flat, flat.T, preferred_element_type=jnp.float32)
    lagged = lag_sum(local_hours, lag_offsets, width) * (1.0 / (lag_offsets.shape[0] * nmodes * columns))
    place = lax.axis_index("co") * 16 + lax.axis_index("x") * 4 + lax.axis_index("y")
    pieces = lagged.reshape(32, width // 32, width)
    summed = sum_pieces(pieces[jnp.arange(32) ^ place])
    low_rank = truncate(place.reshape(1), summed, time_start)
    return (level_basis.T, low_rank)


def solution(mesh):
    fine = Mesh(mesh.devices.reshape(SIZES), AXES)
    return jax.shard_map(
        body,
        mesh=fine,
        in_specs=(P(AXES, None, None), P(), P(), P()),
        out_specs=(P(), P()),
        check_vma=False,
    )
```

```python
import functools
import jax
import jax.numpy as jnp
from jax import lax
from jax.experimental import pallas as pl
from jax.experimental.pallas import tpu as pltpu
from jax.sharding import Mesh, PartitionSpec as P

AXES = ("zl", "co", "y", "zh", "x")
SIZES = (2, 2, 4, 4, 4)
HIGH = lax.Precision.HIGHEST
LANES = 128
ITERS = 3

def dot(a, b, dims=((1,), (0,)), precision=HIGH):
    return lax.dot_general(a, b, (dims, ((), ())), precision=precision, preferred_element_type=jnp.float32)


def split(x):
    hi = x.astype(jnp.bfloat16)
    rest = x - hi.astype(jnp.float32)
    mid = rest.astype(jnp.bfloat16)
    low = (rest - mid.astype(jnp.float32)).astype(jnp.bfloat16)
    return hi, mid, low


def across(row):
    return jnp.broadcast_to(row, (8, LANES))


def inverse_cholesky(gram, out_ref):
    n = gram.shape[0]
    tiles = n // 8
    lane = lax.broadcasted_iota(jnp.int32, (8, LANES), 1)
    sub = lax.broadcasted_iota(jnp.int32, (8, LANES), 0)
    left = [gram[8 * t : 8 * t + 8, :] for t in range(tiles)]
    right = [jnp.where(lane == sub + 8 * t, 1.0, 0.0) for t in range(tiles)]
    for i in range(0, n, 4):
        here, off = i // 8, i % 8
        cols = [
            {t: jnp.broadcast_to(left[t][:, i + k : i + k + 1], (8, LANES)) for t in range(here, tiles)}
            for k in range(4)
        ]
        entry = lambda r, k: across(cols[k][here][off + r : off + r + 1, :])
        low, inv = {}, []
        for k in range(4):
            for r in range(k, 4):
                v = entry(r, k)
                for q in range(k):
                    v = v - low[r, q] * low[k, q]
                if r == k:
                    inv.append(lax.rsqrt(v))
                else:
                    low[r, k] = v * inv[k]
        rows = []
        for k in range(4):
            a = across(left[here][off + k : off + k + 1, :])
            b = across(right[here][off + k : off + k + 1, :])
            for q in range(k):
                a = a - low[k, q] * rows[q][0]
                b = b - low[k, q] * rows[q][1]
            rows.append((a * inv[k], b * inv[k]))
            out_ref[i + k : i + k + 1, :] = rows[k][1][0:1, :]
        for t in range(here + (off > 0), tiles):
            mult = []
            for k in range(4):
                v = cols[k][t]
                for q in range(k):
                    v = v - mult[q] * low[k, q]
                mult.append(v * inv[k])
            for k in range(4):
                left[t] = left[t] - mult[k] * rows[k][0]
                right[t] = right[t] - mult[k] * rows[k][1]


def truncate_kernel(place_ref, *refs):
    pieces, (start_ref, out_ref, d_ref, half_ref, split_ref, z_ref, w_ref, linv_ref) = refs[:10], refs[10:]
    high = pieces[0].shape[1]
    width = d_ref.shape[0]
    held = [(x, y) for x in (0, 1, 3) for y in range(4)], [(2, 0), (2, 1)], [(2, 2), (2, 3)]
    held = held[0][:4], held[0][4:8], held[0][8:], held[1], held[2]
    for c in range(2):
        for ref, stored in zip(pieces[5 * c : 5 * c + 5], held):
            for k, (x, y) in enumerate(stored):
                piece = lax.bitwise_xor(16 * c + 4 * x + y, place_ref[0])
                half_ref[pl.ds(pl.multiple_of(piece * high, 8), high), :] = ref[k]
    blocks = width // LANES
    for i in range(blocks):
        for d in range(4):
            j = (i + d) % blocks
            block = half_ref[LANES * i : LANES * (i + 1), LANES * d : LANES * (d + 1)]
            d_ref[LANES * i : LANES * (i + 1), LANES * j : LANES * (j + 1)] = block
            if d in (1, 2):
                d_ref[LANES * j : LANES * (j + 1), LANES * i : LANES * (i + 1)] = block.T
    lagged = d_ref[...]
    rows = jnp.sum(lagged, axis=1, keepdims=True) * (1.0 / width)
    cols = jnp.sum(lagged, axis=0, keepdims=True) * (1.0 / width)
    mean = jnp.sum(rows, axis=0, keepdims=True) * (1.0 / width)
    debiased = lagged - rows - cols + mean
    for k, part in enumerate(split(debiased)):
        split_ref[k] = part

    def times(x):
        n = x.shape[0]
        parts = jnp.concatenate(split(x), axis=0)
        by = lambda m, k: dot(parts[: m * n], split_ref[k], precision=None)
        one, two, three = by(3, 0), by(2, 1), by(1, 2)
        small = one[2 * n :] + two[n:] + three
        return one[:n] + ((one[n : 2 * n] + two[:n]) + small)

    z_ref[...] = times(start_ref[...].T)

    def step(_, carry):
        z = z_ref[...]
        inverse_cholesky(dot(z, z, ((1,), (1,))), linv_ref)
        w_ref[...] = times(z)
        @pl.when(_ < ITERS - 1)
        def _more():
            z_ref[...] = dot(linv_ref[...], w_ref[...])
        return carry

    lax.fori_loop(0, ITERS, step, 0)
    linv = linv_ref[...]
    basis = dot(linv, z_ref[...])
    inner = dot(dot(linv, w_ref[...]), basis, ((1,), (1,)))
    out_ref[...] = dot(basis, dot(inner, basis), ((0,), (0,)))


def truncate(place, pieces, start):
    width, rank = start.shape
    f32 = jnp.float32
    vm = pl.BlockSpec(memory_space=pltpu.VMEM)
    return pl.pallas_call(
        truncate_kernel,
        out_shape=jax.ShapeDtypeStruct((width, width), f32),
        in_specs=[pl.BlockSpec(memory_space=pltpu.SMEM)] + [vm] * (len(pieces) + 1),
        out_specs=vm,
        scratch_shapes=[
            pltpu.VMEM((width, width), f32),
            pltpu.VMEM((width, 4 * LANES), f32),
            pltpu.VMEM((3, width, width), jnp.bfloat16),
            pltpu.VMEM((rank, width), f32),
            pltpu.VMEM((rank, width), f32),
            pltpu.VMEM((rank, rank), f32),
        ],
        compiler_params=pltpu.CompilerParams(vmem_limit_bytes=48 * 2**20),
        name="truncate",
    )(place, *pieces, start)


def spread(levels, hours, turned=False):
    shape = (levels * hours, levels) if turned else (levels, levels * hours)
    place = lax.broadcasted_iota(jnp.int32, shape, 0 if turned else 1)
    level = lax.broadcasted_iota(jnp.int32, shape, 1 if turned else 0)
    return jnp.where((place >= hours * level) & (place < hours * level + hours), 1.0, 0.0).astype(jnp.bfloat16)


def level_gram_kernel(scale, core_ref, field_ref, start_ref, out_ref, flat_ref, acc_ref):
    step = pl.program_id(0)
    levels, hours, chunk = field_ref.shape
    total = levels * hours
    tile = 256

    @pl.when(step == 0)
    def _():
        acc_ref[...] = jnp.zeros_like(acc_ref)

    flat = field_ref[...].reshape(total, chunk)
    flat_ref[...] = flat
    for j in range(0, total, tile):
        wide = min(tile, total - j)
        acc_ref[j:, j : j + wide] += dot(flat[j:], flat[j : j + wide], ((1,), (1,)), None)

    @pl.when(step == pl.num_programs(0) - 1)
    def _():
        row = lax.broadcasted_iota(jnp.int32, (total, total), 0)
        col = lax.broadcasted_iota(jnp.int32, (total, total), 1)
        same_hour = lax.rem(row, hours) == lax.rem(col, hours)
        same_tile = lax.div(row, tile) == lax.div(col, tile)
        half = jnp.where(same_hour, acc_ref[...] * jnp.where(same_tile, 0.5, 1.0), 0.0)
        left = spread(levels, hours)
        right = spread(levels, hours, True)
        over = sum(dot(left, part, precision=None) for part in reversed(split(half)))
        gram = sum(dot(part, right, precision=None) for part in reversed(split(over)))
        z = (dot(start_ref[...], gram) + dot(start_ref[...], gram, ((1,), (1,)))) * scale
        part = out_ref.shape[1]
        for c in range(2):
            out_ref[lax.bitwise_xor(c, core_ref[0])] = z[part * c : part * (c + 1)]


def level_product(core, field, start, scale):
    levels, hours, columns = field.shape
    nmodes = start.shape[0]
    chunk = 1024
    return pl.pallas_call(
        functools.partial(level_gram_kernel, scale),
        grid=(columns // chunk,),
        out_shape=(
            jax.ShapeDtypeStruct((2, nmodes // 2, levels), jnp.float32),
            jax.ShapeDtypeStruct((levels * hours, columns), jnp.bfloat16),
        ),
        in_specs=[
            pl.BlockSpec(memory_space=pltpu.SMEM),
            pl.BlockSpec((levels, hours, chunk), lambda c: (0, 0, c)),
            pl.BlockSpec((nmodes, levels), lambda c: (0, 0)),
        ],
        out_specs=(
            pl.BlockSpec((2, nmodes // 2, levels), lambda c: (0, 0, 0)),
            pl.BlockSpec((levels * hours, chunk), lambda c: (0, c)),
        ),
        scratch_shapes=[pltpu.VMEM((levels * hours, levels * hours), jnp.float32)],
        compiler_params=pltpu.CompilerParams(vmem_limit_bytes=60 * 2**20),
        name="level_product",
    )(core, field, start)


def project_kernel(hours, core_ref, mine_ref, other_ref, flat_ref, basis_ref, out_ref, weight_ref, linv_ref, z_ref):
    total, chunk = flat_ref.shape
    nmodes, levels = z_ref.shape
    f32, bf16 = jnp.float32, jnp.bfloat16

    @pl.when(pl.program_id(0) == 0)
    def _():
        part = nmodes // 2
        z_ref[pl.ds(pl.multiple_of(part * core_ref[0], 8), part), :] = mine_ref[...]
        z_ref[pl.ds(pl.multiple_of(part * (1 - core_ref[0]), 8), part), :] = other_ref[...]
        z = z_ref[...]
        gram = dot(z, z, ((1,), (1,)))
        padded = jnp.concatenate([gram, jnp.zeros((nmodes, LANES - nmodes), f32)], axis=1)
        inverse_cholesky(padded, linv_ref)
        basis = dot(linv_ref[:, :nmodes], z)
        basis_ref[...] = basis
        modes_by_hours = spread(nmodes, hours, True)
        tall = dot(modes_by_hours, basis.astype(bf16), precision=None).astype(bf16)
        wide = dot(tall, spread(levels, hours), precision=None)
        row = lax.broadcasted_iota(jnp.int32, wide.shape, 0)
        col = lax.broadcasted_iota(jnp.int32, wide.shape, 1)
        weight_ref[...] = jnp.where(lax.rem(row, hours) == lax.rem(col, hours), wide, 0.0).astype(bf16)

    made = dot(weight_ref[...], flat_ref[...], precision=None)
    groups, blocks, rows, _ = out_ref.shape
    for a in range(groups):
        for b in range(blocks):
            out_ref[a, b] = made[rows * a : rows * (a + 1), LANES * b : LANES * (b + 1)].astype(bf16)


def project(core, mine, other, flat, hours, groups):
    total, columns = flat.shape
    part, levels = mine.shape
    nmodes = 2 * part
    chunk = 1024
    rows = hours * nmodes // groups
    return pl.pallas_call(
        functools.partial(project_kernel, hours),
        grid=(columns // chunk,),
        out_shape=(
            jax.ShapeDtypeStruct((nmodes, levels), jnp.float32),
            jax.ShapeDtypeStruct((groups, columns // LANES, rows, LANES), jnp.bfloat16),
        ),
        in_specs=[
            pl.BlockSpec(memory_space=pltpu.SMEM),
            pl.BlockSpec((part, levels), lambda c: (0, 0)),
            pl.BlockSpec((part, levels), lambda c: (0, 0)),
            pl.BlockSpec((total, chunk), lambda c: (0, c)),
        ],
        out_specs=(
            pl.BlockSpec((nmodes, levels), lambda c: (0, 0)),
            pl.BlockSpec((groups, chunk // LANES, rows, LANES), lambda c: (0, c, 0, 0)),
        ),
        scratch_shapes=[
            pltpu.VMEM((hours * nmodes, total), jnp.bfloat16),
            pltpu.VMEM((nmodes, LANES), jnp.float32),
            pltpu.VMEM((nmodes, levels), jnp.float32),
        ],
        compiler_params=pltpu.CompilerParams(vmem_limit_bytes=60 * 2**20),
        name="project",
    )(core, mine, other, flat)


def slot(piece):
    c, x, y = piece >> 4, (piece >> 2) & 3, piece & 3
    half = y >> 1
    turn = jnp.where(half == 0, (4 - x) & 3, x)
    return c, half, turn ^ (turn >> 1), y & 1


def hour_gram_kernel(scale, place_ref, lag_ref, got_ref, out_ref, flat_ref, gram_ref, half_ref):
    senders, rows, _ = got_ref.shape
    width = half_ref.shape[0]
    f32, bf16 = jnp.float32, jnp.bfloat16
    hours = flat_ref.shape[0] // senders
    per = rows // hours
    many = 32
    size = many * rows
    new = lax.broadcasted_iota(jnp.int32, (size, size), 0)
    old = lax.broadcasted_iota(jnp.int32, (size, size), 1)
    span = many * hours
    mode, rest = lax.div(new, span), lax.rem(new, span)
    wanted = lax.div(rest, hours) * rows + mode * hours + lax.rem(rest, hours)
    pick = jnp.where(old == wanted, 1.0, 0.0).astype(bf16)
    for s in range(0, senders, 2 * many):
        pair = [got_ref[s + many * k : s + many * (k + 1)].reshape(size, LANES) for k in range(2)]
        moved = dot(pick, jnp.concatenate(pair, axis=1), precision=None).astype(bf16)
        for k in range(2):
            for m in range(per):
                flat_ref[hours * s + span * k : hours * s + span * (k + 1), LANES * m : LANES * (m + 1)] = moved[
                    span * m : span * (m + 1), LANES * k : LANES * (k + 1)
                ]
    for i in range(0, flat_ref.shape[0], 256):
        band = dot(flat_ref[i : i + 256, :], flat_ref[...], ((1,), (1,)), None)
        for b in range(gram_ref.shape[0]):
            gram_ref[b, i : i + 256, :] = band[:, LANES * b : LANES * (b + 1)]

    blocks = width // LANES
    lane = lax.broadcasted_iota(jnp.int32, (LANES, LANES), 1)
    for i in range(blocks):
        wanted = [(i + d) % blocks for d in range(4)]

        def add(j, acc):
            offset = lag_ref[j]
            whole, part = lax.div(offset, LANES), lax.rem(offset, LANES)
            turn = lax.rem(LANES - part, LANES)
            at = offset + LANES * i
            load = {}
            for b in sorted(set(wanted) | {w + 1 for w in wanted}):
                column = jnp.minimum(whole + b, gram_ref.shape[0] - 1)
                load[b] = pltpu.roll(gram_ref[column, pl.ds(at, LANES), :], turn, 1)
            return tuple(a + jnp.where(lane < LANES - part, load[w], load[w + 1]) for a, w in zip(acc, wanted))

        acc = lax.fori_loop(0, lag_ref.shape[0], add, tuple(jnp.zeros((LANES, LANES), f32) for _ in wanted))
        for d in range(4):
            half_ref[LANES * i : LANES * (i + 1), LANES * d : LANES * (d + 1)] = acc[d] * scale
    high = out_ref.shape[4]
    for p in range(width // high):
        c, h, x, y = slot(lax.bitwise_xor(p, place_ref[0]))
        out_ref[c, h, x, y] = half_ref[high * p : high * (p + 1), :]


def hour_gram(place, lags, got, width, hours, scale):
    senders, rows, _ = got.shape
    total = senders * hours
    wide = 4 * LANES
    smem, vm = pl.BlockSpec(memory_space=pltpu.SMEM), pl.BlockSpec(memory_space=pltpu.VMEM)
    return pl.pallas_call(
        functools.partial(hour_gram_kernel, scale),
        out_shape=jax.ShapeDtypeStruct((2, 2, 4, 2, width // 32, wide), jnp.float32),
        in_specs=[smem, smem, vm],
        out_specs=vm,
        scratch_shapes=[
            pltpu.VMEM((total, rows // hours * LANES), jnp.bfloat16),
            pltpu.VMEM((total // LANES, total, LANES), jnp.float32),
            pltpu.VMEM((width, wide), jnp.float32),
        ],
        compiler_params=pltpu.CompilerParams(vmem_limit_bytes=48 * 2**20),
        name="hour_gram",
    )(place, lags, got)


def swap(x, axis, k):
    n = SIZES[AXES.index(axis)]
    return lax.ppermute(x, axis, [(i, i ^ k) for i in range(n)])


def all_sum(x, axis):
    got = [swap(x, axis, k) for k in (1, 2, 3)]
    return (x + got[0]) + (got[1] + got[2])


def sum_pieces(pieces):
    x = pieces[0] + swap(pieces[1], "co", 1)
    left, right = x[0], x[1]
    left, right = left[:2] + swap(left[2:], "x", 1), right[:2] + swap(right[2:], "x", 3)
    left, right = left[0] + swap(left[1], "x", 3), right[0] + swap(right[1], "x", 1)
    got = [swap(part, "y", k) for k, part in ((1, left[1]), (2, right[0]), (3, right[1]))]
    mine = (left[0] + got[0]) + (got[1] + got[2])
    mine = mine + swap(mine, "zl", 1)
    mine = all_sum(mine, "zh")
    mine = jnp.stack([mine] + [swap(mine, "y", k) for k in (1, 2, 3)])
    one, three = swap(mine, "x", 1), swap(mine, "x", 3)
    held = [mine, one, three, swap(one[:2], "x", 3), swap(three[2:], "x", 1)]
    return held + [swap(part, "co", 1) for part in held]


def body(field, level_start, time_start, lag_offsets):
    hour_count, levels, columns = field.shape
    devices = lax.axis_size(AXES)
    hours_all = hour_count * devices
    width = time_start.shape[0]
    nmodes = level_start.shape[1]
    core = lax.axis_index("co").reshape(1)
    place = core * 16 + lax.axis_index("x") * 4 + lax.axis_index("y")
    scale = 1.0 / (hours_all * columns)
    halves, level_hours = level_product(core, jnp.transpose(field, (1, 0, 2)), level_start.T, scale)
    z = halves[0] + swap(halves[1], "co", 1)
    z = z + swap(z, "zl", 1)
    for axis in ("x", "y", "zh"):
        z = all_sum(z, axis)
    level_basis, sent = project(core, z, swap(z, "co", 1), level_hours, hour_count, 8)
    sent = sent.reshape(devices, 24, LANES)
    received = lax.all_to_all(sent, AXES, split_axis=0, concat_axis=0, tiled=True)
    scale = 1.0 / (lag_offsets.shape[0] * nmodes * columns)
    pieces = hour_gram(place, lag_offsets, received, width, hour_count, scale)
    low_rank = truncate(place, sum_pieces(pieces), time_start)
    return (level_basis.T, low_rank)


def solution(mesh):
    fine = Mesh(mesh.devices.reshape(SIZES), AXES)
    return jax.shard_map(
        body,
        mesh=fine,
        in_specs=(P(AXES, None, None), P(), P(), P()),
        out_specs=(P(), P()),
        check_vma=False,
    )
```

```python
import functools
import jax
import jax.numpy as jnp
from jax import lax
from jax.experimental import pallas as pl
from jax.experimental.pallas import tpu as pltpu
from jax.sharding import Mesh, PartitionSpec as P

AXES = ("zl", "co", "y", "zh", "x")
SIZES = (2, 2, 4, 4, 4)
HIGH = lax.Precision.HIGHEST
LANES = 128
ITERS = 3

def dot(a, b, dims=((1,), (0,)), precision=HIGH):
    return lax.dot_general(a, b, (dims, ((), ())), precision=precision, preferred_element_type=jnp.float32)


def split(x):
    hi = x.astype(jnp.bfloat16)
    rest = x - hi.astype(jnp.float32)
    mid = rest.astype(jnp.bfloat16)
    low = (rest - mid.astype(jnp.float32)).astype(jnp.bfloat16)
    return hi, mid, low


def across(row):
    return jnp.broadcast_to(row, (8, LANES))


def inverse_cholesky(gram, out_ref):
    n = gram.shape[0]
    tiles = n // 8
    lane = lax.broadcasted_iota(jnp.int32, (8, LANES), 1)
    sub = lax.broadcasted_iota(jnp.int32, (8, LANES), 0)
    left = [gram[8 * t : 8 * t + 8, :] for t in range(tiles)]
    right = [jnp.where(lane == sub + 8 * t, 1.0, 0.0) for t in range(tiles)]
    for i in range(0, n, 4):
        here, off = i // 8, i % 8
        cols = [
            {t: jnp.broadcast_to(left[t][:, i + k : i + k + 1], (8, LANES)) for t in range(here, tiles)}
            for k in range(4)
        ]
        entry = lambda r, k: across(cols[k][here][off + r : off + r + 1, :])
        low, inv = {}, []
        for k in range(4):
            for r in range(k, 4):
                v = entry(r, k)
                for q in range(k):
                    v = v - low[r, q] * low[k, q]
                if r == k:
                    inv.append(lax.rsqrt(v))
                else:
                    low[r, k] = v * inv[k]
        rows = []
        for k in range(4):
            a = across(left[here][off + k : off + k + 1, :])
            b = across(right[here][off + k : off + k + 1, :])
            for q in range(k):
                a = a - low[k, q] * rows[q][0]
                b = b - low[k, q] * rows[q][1]
            rows.append((a * inv[k], b * inv[k]))
            out_ref[i + k : i + k + 1, :] = rows[k][1][0:1, :]
        for t in range(here + (off > 0), tiles):
            mult = []
            for k in range(4):
                v = cols[k][t]
                for q in range(k):
                    v = v - mult[q] * low[k, q]
                mult.append(v * inv[k])
            for k in range(4):
                left[t] = left[t] - mult[k] * rows[k][0]
                right[t] = right[t] - mult[k] * rows[k][1]


def truncate_kernel(core_ref, mine_ref, other_ref, start_ref, out_ref, d_ref, half_ref, split_ref, z_ref, w_ref, linv_ref):
    each, high, _ = mine_ref.shape
    width = d_ref.shape[0]
    for ref, core in ((mine_ref, core_ref[0]), (other_ref, 1 - core_ref[0])):
        for k in range(each):
            half_ref[pl.ds(pl.multiple_of((core * each + k) * high, 8), high), :] = ref[k]
    blocks = width // LANES
    for i in range(blocks):
        for d in range(4):
            j = (i + d) % blocks
            block = half_ref[LANES * i : LANES * (i + 1), LANES * d : LANES * (d + 1)]
            d_ref[LANES * i : LANES * (i + 1), LANES * j : LANES * (j + 1)] = block
            if d in (1, 2):
                d_ref[LANES * j : LANES * (j + 1), LANES * i : LANES * (i + 1)] = block.T
    lagged = d_ref[...]
    rows = jnp.sum(lagged, axis=1, keepdims=True) * (1.0 / width)
    cols = jnp.sum(lagged, axis=0, keepdims=True) * (1.0 / width)
    mean = jnp.sum(rows, axis=0, keepdims=True) * (1.0 / width)
    debiased = lagged - rows - cols + mean
    for k, part in enumerate(split(debiased)):
        split_ref[k] = part

    def times(x):
        n = x.shape[0]
        parts = jnp.concatenate(split(x), axis=0)
        by = lambda m, k: dot(parts[: m * n], split_ref[k], precision=None)
        one, two, three = by(3, 0), by(2, 1), by(1, 2)
        small = one[2 * n :] + two[n:] + three
        return one[:n] + ((one[n : 2 * n] + two[:n]) + small)

    z_ref[...] = times(start_ref[...].T)

    def step(_, carry):
        z = z_ref[...]
        inverse_cholesky(dot(z, z, ((1,), (1,))), linv_ref)
        w_ref[...] = times(z)
        @pl.when(_ < ITERS - 1)
        def _more():
            z_ref[...] = dot(linv_ref[...], w_ref[...])
        return carry

    lax.fori_loop(0, ITERS, step, 0)
    linv = linv_ref[...]
    basis = dot(linv, z_ref[...])
    inner = dot(dot(linv, w_ref[...]), basis, ((1,), (1,)))
    out_ref[...] = dot(basis, dot(inner, basis), ((0,), (0,)))


def truncate(core, mine, other, start):
    width, rank = start.shape
    f32 = jnp.float32
    vm = pl.BlockSpec(memory_space=pltpu.VMEM)
    return pl.pallas_call(
        truncate_kernel,
        out_shape=jax.ShapeDtypeStruct((width, width), f32),
        in_specs=[pl.BlockSpec(memory_space=pltpu.SMEM), vm, vm, vm],
        out_specs=vm,
        scratch_shapes=[
            pltpu.VMEM((width, width), f32),
            pltpu.VMEM((width, 4 * LANES), f32),
            pltpu.VMEM((3, width, width), jnp.bfloat16),
            pltpu.VMEM((rank, width), f32),
            pltpu.VMEM((rank, width), f32),
            pltpu.VMEM((rank, rank), f32),
        ],
        compiler_params=pltpu.CompilerParams(vmem_limit_bytes=48 * 2**20),
        name="truncate",
    )(core, mine, other, start)


def counted(shape, axis):
    return lax.broadcasted_iota(jnp.int32, shape, axis)


def spread(levels, hours, turned=False):
    if turned:
        place, level = counted((levels * hours, 1), 0), counted((1, levels), 1)
    else:
        place, level = counted((1, levels * hours), 1), counted((levels, 1), 0)
    first = level * hours
    return jnp.where((place >= first) & (place < first + hours), 1.0, 0.0).astype(jnp.bfloat16)


def same(rows, columns, of):
    return of(counted((rows, 1), 0)) == of(counted((1, columns), 1))


def level_gram_kernel(scale, core_ref, field_ref, start_ref, out_ref, flat_ref, acc_ref):
    step = pl.program_id(0)
    levels, hours, chunk = field_ref.shape
    total = levels * hours
    tile = 256

    @pl.when(step == 0)
    def _():
        acc_ref[...] = jnp.zeros_like(acc_ref)

    flat = field_ref[...].reshape(total, chunk)
    flat_ref[...] = flat
    for j in range(0, total, tile):
        wide = min(tile, total - j)
        acc_ref[j:, j : j + wide] += dot(flat[j:], flat[j : j + wide], ((1,), (1,)), None)

    @pl.when(step == pl.num_programs(0) - 1)
    def _():
        weight = jnp.where(same(total, total, lambda i: lax.div(i, tile)), 0.5, 1.0)
        weight = jnp.where(same(total, total, lambda i: lax.rem(i, hours)), weight, 0.0)
        half = acc_ref[...] * weight
        left = spread(levels, hours)
        right = spread(levels, hours, True)
        over = sum(dot(left, part, precision=None) for part in reversed(split(half)))
        gram = sum(dot(part, right, precision=None) for part in reversed(split(over)))
        z = (dot(start_ref[...], gram) + dot(start_ref[...], gram, ((1,), (1,)))) * scale
        part = out_ref.shape[1]
        for c in range(2):
            out_ref[lax.bitwise_xor(c, core_ref[0])] = z[part * c : part * (c + 1)]


def level_product(core, field, start, scale):
    levels, hours, columns = field.shape
    nmodes = start.shape[0]
    chunk = 1024
    return pl.pallas_call(
        functools.partial(level_gram_kernel, scale),
        grid=(columns // chunk,),
        out_shape=(
            jax.ShapeDtypeStruct((2, nmodes // 2, levels), jnp.float32),
            jax.ShapeDtypeStruct((levels * hours, columns), jnp.bfloat16),
        ),
        in_specs=[
            pl.BlockSpec(memory_space=pltpu.SMEM),
            pl.BlockSpec((levels, hours, chunk), lambda c: (0, 0, c)),
            pl.BlockSpec((nmodes, levels), lambda c: (0, 0)),
        ],
        out_specs=(
            pl.BlockSpec((2, nmodes // 2, levels), lambda c: (0, 0, 0)),
            pl.BlockSpec((levels * hours, chunk), lambda c: (0, c)),
        ),
        scratch_shapes=[pltpu.VMEM((levels * hours, levels * hours), jnp.float32)],
        compiler_params=pltpu.CompilerParams(vmem_limit_bytes=60 * 2**20),
        name="level_product",
    )(core, field, start)


def project_kernel(hours, core_ref, mine_ref, other_ref, flat_ref, basis_ref, out_ref, weight_ref, linv_ref, z_ref):
    total, chunk = flat_ref.shape
    nmodes, levels = z_ref.shape
    f32, bf16 = jnp.float32, jnp.bfloat16

    @pl.when(pl.program_id(0) == 0)
    def _():
        part = nmodes // 2
        z_ref[pl.ds(pl.multiple_of(part * core_ref[0], 8), part), :] = mine_ref[...]
        z_ref[pl.ds(pl.multiple_of(part * (1 - core_ref[0]), 8), part), :] = other_ref[...]
        z = z_ref[...]
        gram = dot(z, z, ((1,), (1,)))
        padded = jnp.concatenate([gram, jnp.zeros((nmodes, LANES - nmodes), f32)], axis=1)
        inverse_cholesky(padded, linv_ref)
        basis = dot(linv_ref[:, :nmodes], z)
        basis_ref[...] = basis
        modes_by_hours = spread(nmodes, hours, True)
        tall = dot(modes_by_hours, basis.astype(bf16), precision=None).astype(bf16)
        wide = dot(tall, spread(levels, hours), precision=None)
        weight_ref[...] = jnp.where(same(*wide.shape, lambda i: lax.rem(i, hours)), wide, 0.0).astype(bf16)

    made = dot(weight_ref[...], flat_ref[...], precision=None)
    groups, blocks, rows, _ = out_ref.shape
    for a in range(groups):
        for b in range(blocks):
            out_ref[a, b] = made[rows * a : rows * (a + 1), LANES * b : LANES * (b + 1)].astype(bf16)


def project(core, mine, other, flat, hours, groups):
    total, columns = flat.shape
    part, levels = mine.shape
    nmodes = 2 * part
    chunk = 1024
    rows = hours * nmodes // groups
    return pl.pallas_call(
        functools.partial(project_kernel, hours),
        grid=(columns // chunk,),
        out_shape=(
            jax.ShapeDtypeStruct((nmodes, levels), jnp.float32),
            jax.ShapeDtypeStruct((groups, columns // LANES, rows, LANES), jnp.bfloat16),
        ),
        in_specs=[
            pl.BlockSpec(memory_space=pltpu.SMEM),
            pl.BlockSpec((part, levels), lambda c: (0, 0)),
            pl.BlockSpec((part, levels), lambda c: (0, 0)),
            pl.BlockSpec((total, chunk), lambda c: (0, c)),
        ],
        out_specs=(
            pl.BlockSpec((nmodes, levels), lambda c: (0, 0)),
            pl.BlockSpec((groups, chunk // LANES, rows, LANES), lambda c: (0, c, 0, 0)),
        ),
        scratch_shapes=[
            pltpu.VMEM((hours * nmodes, total), jnp.bfloat16),
            pltpu.VMEM((nmodes, LANES), jnp.float32),
            pltpu.VMEM((nmodes, levels), jnp.float32),
        ],
        compiler_params=pltpu.CompilerParams(vmem_limit_bytes=60 * 2**20),
        name="project",
    )(core, mine, other, flat)


def hour_gram_kernel(scale, core_ref, lag_ref, got_ref, out_ref, flat_ref, gram_ref, half_ref):
    senders, rows, _ = got_ref.shape
    width = half_ref.shape[0]
    f32, bf16 = jnp.float32, jnp.bfloat16
    hours = flat_ref.shape[0] // senders
    per = rows // hours
    many = 32
    size = many * rows
    new = counted((size, 1), 0)
    span = many * hours
    mode, rest = lax.div(new, span), lax.rem(new, span)
    wanted = lax.div(rest, hours) * rows + mode * hours + lax.rem(rest, hours)
    pick = jnp.where(counted((1, size), 1) == wanted, 1.0, 0.0).astype(bf16)
    for s in range(0, senders, 2 * many):
        pair = [got_ref[s + many * k : s + many * (k + 1)].reshape(size, LANES) for k in range(2)]
        moved = dot(pick, jnp.concatenate(pair, axis=1), precision=None).astype(bf16)
        for k in range(2):
            for m in range(per):
                flat_ref[hours * s + span * k : hours * s + span * (k + 1), LANES * m : LANES * (m + 1)] = moved[
                    span * m : span * (m + 1), LANES * k : LANES * (k + 1)
                ]
    for i in range(0, flat_ref.shape[0], 256):
        band = dot(flat_ref[i : i + 256, :], flat_ref[...], ((1,), (1,)), None)
        for b in range(gram_ref.shape[0]):
            gram_ref[b, i : i + 256, :] = band[:, LANES * b : LANES * (b + 1)]

    blocks = width // LANES
    lane = lax.broadcasted_iota(jnp.int32, (LANES, LANES), 1)
    for i in range(blocks):
        wanted = [(i + d) % blocks for d in range(4)]

        def add(j, acc):
            offset = lag_ref[j]
            whole, part = lax.div(offset, LANES), lax.rem(offset, LANES)
            turn = lax.rem(LANES - part, LANES)
            at = offset + LANES * i
            load = {}
            for b in sorted(set(wanted) | {w + 1 for w in wanted}):
                column = jnp.minimum(whole + b, gram_ref.shape[0] - 1)
                load[b] = pltpu.roll(gram_ref[column, pl.ds(at, LANES), :], turn, 1)
            return tuple(a + jnp.where(lane < LANES - part, load[w], load[w + 1]) for a, w in zip(acc, wanted))

        acc = lax.fori_loop(0, lag_ref.shape[0], add, tuple(jnp.zeros((LANES, LANES), f32) for _ in wanted))
        for d in range(4):
            half_ref[LANES * i : LANES * (i + 1), LANES * d : LANES * (d + 1)] = acc[d] * scale
    _, each, high, _ = out_ref.shape
    for c in range(2):
        for k in range(each):
            at = (c * each + k) * high
            out_ref[lax.bitwise_xor(c, core_ref[0]), k] = half_ref[at : at + high, :]


def hour_gram(core, lags, got, width, hours, scale):
    senders, rows, _ = got.shape
    total = senders * hours
    wide = 4 * LANES
    smem, vm = pl.BlockSpec(memory_space=pltpu.SMEM), pl.BlockSpec(memory_space=pltpu.VMEM)
    return pl.pallas_call(
        functools.partial(hour_gram_kernel, scale),
        out_shape=jax.ShapeDtypeStruct((2, 16, width // 32, wide), jnp.float32),
        in_specs=[smem, smem, vm],
        out_specs=vm,
        scratch_shapes=[
            pltpu.VMEM((total, rows // hours * LANES), jnp.bfloat16),
            pltpu.VMEM((total // LANES, total, LANES), jnp.float32),
            pltpu.VMEM((width, wide), jnp.float32),
        ],
        compiler_params=pltpu.CompilerParams(vmem_limit_bytes=48 * 2**20),
        name="hour_gram",
    )(core, lags, got)


PLANE = ("y", "x")
COLUMN = ("zl", "zh")


def other_core(x):
    return lax.ppermute(x, "co", [(0, 1), (1, 0)])


def exchange(x, axes):
    return lax.all_to_all(x, axes, split_axis=0, concat_axis=0, tiled=True)


def collect(x, axes):
    return exchange(jnp.broadcast_to(x, (lax.axis_size(axes),) + x.shape), axes)


def sum_over(x, axes):
    return jnp.sum(collect(x, axes), axis=0)


def sum_pieces(pieces):
    here = pieces[0] + other_core(pieces[1])
    mine = jnp.sum(exchange(here, PLANE), axis=0)
    return collect(sum_over(mine, COLUMN), PLANE)


def body(field, level_start, time_start, lag_offsets):
    hour_count, levels, columns = field.shape
    devices = lax.axis_size(AXES)
    hours_all = hour_count * devices
    width = time_start.shape[0]
    nmodes = level_start.shape[1]
    core = lax.axis_index("co").reshape(1)
    scale = 1.0 / (hours_all * columns)
    halves, level_hours = level_product(core, jnp.transpose(field, (1, 0, 2)), level_start.T, scale)
    z = halves[0] + other_core(halves[1])
    z = sum_over(sum_over(z, PLANE), COLUMN)
    level_basis, sent = project(core, z, other_core(z), level_hours, hour_count, 8)
    sent = sent.reshape(devices, 24, LANES)
    received = exchange(sent, AXES)
    scale = 1.0 / (lag_offsets.shape[0] * nmodes * columns)
    summed = sum_pieces(hour_gram(core, lag_offsets, received, width, hour_count, scale))
    low_rank = truncate(core, summed, other_core(summed), time_start)
    return (level_basis.T, low_rank)


def solution(mesh):
    fine = Mesh(mesh.devices.reshape(SIZES), AXES)
    return jax.shard_map(
        body,
        mesh=fine,
        in_specs=(P(AXES, None, None), P(), P(), P()),
        out_specs=(P(), P()),
        check_vma=False,
    )
```

```python
import functools
import jax
import jax.numpy as jnp
from jax import lax
from jax.experimental import pallas as pl
from jax.experimental.pallas import tpu as pltpu
from jax.sharding import Mesh, PartitionSpec as P

AXES = ("zl", "co", "y", "zh", "x")
SIZES = (2, 2, 4, 4, 4)
HIGH = lax.Precision.HIGHEST
LANES = 128
ITERS = 3

def dot(a, b, dims=((1,), (0,)), precision=HIGH):
    return lax.dot_general(a, b, (dims, ((), ())), precision=precision, preferred_element_type=jnp.float32)


def split(x):
    hi = x.astype(jnp.bfloat16)
    rest = x - hi.astype(jnp.float32)
    mid = rest.astype(jnp.bfloat16)
    low = (rest - mid.astype(jnp.float32)).astype(jnp.bfloat16)
    return hi, mid, low


def across(row):
    return jnp.broadcast_to(row, (8, LANES))


def inverse_cholesky(gram, out_ref):
    n = gram.shape[0]
    tiles = n // 8
    lane = lax.broadcasted_iota(jnp.int32, (8, LANES), 1)
    sub = lax.broadcasted_iota(jnp.int32, (8, LANES), 0)
    left = [gram[8 * t : 8 * t + 8, :] for t in range(tiles)]
    right = [jnp.where(lane == sub + 8 * t, 1.0, 0.0) for t in range(tiles)]
    for here in range(tiles):
        cols = [
            {
                t: jnp.broadcast_to(left[t][:, 8 * here + k : 8 * here + k + 1], (8, LANES))
                for t in range(here, tiles)
            }
            for k in range(8)
        ]
        entry = {(r, k): across(cols[k][here][r : r + 1, :]) for k in range(8) for r in range(k, 8)}
        low, inv = {}, []
        for k in range(8):
            inv.append(lax.rsqrt(entry[k, k]))
            for r in range(k + 1, 8):
                low[r, k] = entry[r, k] * inv[k]
            for q in range(k + 1, 8):
                for r in range(q, 8):
                    entry[r, q] = entry[r, q] - low[r, k] * low[q, k]
        side = [across(left[here][k : k + 1, :]) for k in range(8)], [across(right[here][k : k + 1, :]) for k in range(8)]
        for k in range(8):
            for row in side:
                row[k] = row[k] * inv[k]
                for r in range(k + 1, 8):
                    row[r] = row[r] - low[r, k] * row[k]
            out_ref[8 * here + k : 8 * here + k + 1, :] = side[1][k][0:1, :]
        for t in range(here + 1, tiles):
            mult = [cols[k][t] for k in range(8)]
            for k in range(8):
                mult[k] = mult[k] * inv[k]
                for r in range(k + 1, 8):
                    mult[r] = mult[r] - mult[k] * low[r, k]
                left[t] = left[t] - mult[k] * side[0][k]
                right[t] = right[t] - mult[k] * side[1][k]


def truncate_kernel(core_ref, mine_ref, other_ref, start_ref, out_ref, d_ref, half_ref, split_ref, z_ref, w_ref, linv_ref):
    each, high, _ = mine_ref.shape
    width = d_ref.shape[0]
    for ref, core in ((mine_ref, core_ref[0]), (other_ref, 1 - core_ref[0])):
        for k in range(each):
            half_ref[pl.ds(pl.multiple_of((core * each + k) * high, 8), high), :] = ref[k]
    blocks = width // LANES
    for i in range(blocks):
        for d in range(4):
            j = (i + d) % blocks
            block = half_ref[LANES * i : LANES * (i + 1), LANES * d : LANES * (d + 1)]
            d_ref[LANES * i : LANES * (i + 1), LANES * j : LANES * (j + 1)] = block
            if d in (1, 2):
                d_ref[LANES * j : LANES * (j + 1), LANES * i : LANES * (i + 1)] = block.T
    lagged = d_ref[...]
    rows = jnp.sum(lagged, axis=1, keepdims=True) * (1.0 / width)
    cols = jnp.sum(lagged, axis=0, keepdims=True) * (1.0 / width)
    mean = jnp.sum(rows, axis=0, keepdims=True) * (1.0 / width)
    debiased = lagged - rows - cols + mean
    for k, part in enumerate(split(debiased)):
        split_ref[k] = part

    def times(x):
        n = x.shape[0]
        parts = jnp.concatenate(split(x), axis=0)
        by = lambda m, k: dot(parts[: m * n], split_ref[k], precision=None)
        one, two, three = by(3, 0), by(2, 1), by(1, 2)
        small = one[2 * n :] + two[n:] + three
        return one[:n] + ((one[n : 2 * n] + two[:n]) + small)

    z_ref[...] = times(start_ref[...].T)

    def step(_, carry):
        z = z_ref[...]
        inverse_cholesky(dot(z, z, ((1,), (1,))), linv_ref)
        w_ref[...] = times(z)
        @pl.when(_ < ITERS - 1)
        def _more():
            z_ref[...] = dot(linv_ref[...], w_ref[...])
        return carry

    lax.fori_loop(0, ITERS, step, 0)
    linv = linv_ref[...]
    basis = dot(linv, z_ref[...])
    inner = dot(dot(linv, w_ref[...]), basis, ((1,), (1,)))
    out_ref[...] = dot(basis, dot(inner, basis), ((0,), (0,)), lax.Precision.HIGH)


def truncate(core, mine, other, start):
    width, rank = start.shape
    f32 = jnp.float32
    vm = pl.BlockSpec(memory_space=pltpu.VMEM)
    return pl.pallas_call(
        truncate_kernel,
        out_shape=jax.ShapeDtypeStruct((width, width), f32),
        in_specs=[pl.BlockSpec(memory_space=pltpu.SMEM), vm, vm, vm],
        out_specs=vm,
        scratch_shapes=[
            pltpu.VMEM((width, width), f32),
            pltpu.VMEM((width, 4 * LANES), f32),
            pltpu.VMEM((3, width, width), jnp.bfloat16),
            pltpu.VMEM((rank, width), f32),
            pltpu.VMEM((rank, width), f32),
            pltpu.VMEM((rank, rank), f32),
        ],
        compiler_params=pltpu.CompilerParams(vmem_limit_bytes=48 * 2**20),
        name="truncate",
    )(core, mine, other, start)


def counted(shape, axis):
    return lax.broadcasted_iota(jnp.int32, shape, axis)


def spread(levels, hours, places, turned=False):
    if turned:
        place, level = counted((places, 1), 0), counted((1, levels), 1)
    else:
        place, level = counted((1, places), 1), counted((levels, 1), 0)
    first = level * hours
    return jnp.where((place >= first) & (place < first + hours), 1.0, 0.0).astype(jnp.bfloat16)


def same(rows, columns, of):
    return of(counted((rows, 1), 0)) == of(counted((1, columns), 1))


def level_gram_kernel(scale, core_ref, field_ref, start_ref, out_ref, flat_ref, acc_ref, field_vmem, flat_vmem, sems, flat_sems):
    levels, hours, columns = field_ref.shape
    total = flat_ref.shape[0]
    chunk = columns // sems.shape[0]
    tile = 256
    copies, writes = [], []
    for c in range(sems.shape[0]):
        at = pl.ds(c * chunk, chunk)
        copies.append(pltpu.make_async_copy(field_ref.at[:, :, at], field_vmem.at[:, :, at], sems.at[c]))
        copies[c].start()
    for c, copy in enumerate(copies):
        copy.wait()
        flat = field_vmem[:, :, c * chunk : (c + 1) * chunk].reshape(levels * hours, chunk)
        flat = jnp.concatenate([flat, jnp.zeros((total - levels * hours, chunk), jnp.bfloat16)], axis=0)
        at = pl.ds(c * chunk, chunk)
        flat_vmem[:, at] = flat
        writes.append(pltpu.make_async_copy(flat_vmem.at[:, at], flat_ref.at[:, at], flat_sems.at[c]))
        writes[c].start()
        for j in range(0, total, tile):
            wide = min(tile, total - j)
            block = dot(flat[j:], flat[j : j + wide], ((1,), (1,)), None)
            acc_ref[j:, j : j + wide] = block if c == 0 else acc_ref[j:, j : j + wide] + block
    for j in range(tile, total, tile):
        acc_ref[j - tile : j, j:] = jnp.zeros((tile, total - j), jnp.float32)
    weight = jnp.where(same(total, total, lambda i: lax.div(i, tile)), 0.5, 1.0)
    weight = jnp.where(same(total, total, lambda i: lax.rem(i, hours)), weight, 0.0)
    half = acc_ref[...] * weight
    left = spread(levels, hours, total)
    right = spread(levels, hours, total, True)
    over = sum(dot(left, part, precision=None) for part in reversed(split(half)))
    gram = sum(dot(part, right, precision=None) for part in reversed(split(over)))
    z = (dot(start_ref[...], gram) + dot(start_ref[...], gram, ((1,), (1,)))) * scale
    part = out_ref.shape[1]
    for c in range(2):
        out_ref[lax.bitwise_xor(c, core_ref[0])] = z[part * c : part * (c + 1)]
    for write in writes:
        write.wait()


def level_product(core, field, start, scale):
    levels, hours, columns = field.shape
    nmodes = start.shape[0]
    total = -(-levels * hours // 16) * 16
    smem, vm = pl.BlockSpec(memory_space=pltpu.SMEM), pl.BlockSpec(memory_space=pltpu.VMEM)
    return pl.pallas_call(
        functools.partial(level_gram_kernel, scale),
        out_shape=(
            jax.ShapeDtypeStruct((2, nmodes // 2, levels), jnp.float32),
            jax.ShapeDtypeStruct((total, columns), jnp.bfloat16),
        ),
        in_specs=[smem, pl.BlockSpec(memory_space=pltpu.HBM), vm],
        out_specs=(vm, pl.BlockSpec(memory_space=pltpu.HBM)),
        scratch_shapes=[
            pltpu.VMEM((total, total), jnp.float32),
            pltpu.VMEM((levels, hours, columns), jnp.bfloat16),
            pltpu.VMEM((total, columns), jnp.bfloat16),
            pltpu.SemaphoreType.DMA((4,)),
            pltpu.SemaphoreType.DMA((4,)),
        ],
        compiler_params=pltpu.CompilerParams(vmem_limit_bytes=60 * 2**20),
        name="level_product",
    )(core, field, start)


def project_kernel(hours, core_ref, mine_ref, other_ref, flat_ref, basis_ref, out_ref, weight_ref, linv_ref, z_ref, flat_vmem, sems):
    total, columns = flat_ref.shape
    chunk = columns // sems.shape[0]
    copies = []
    for c in range(sems.shape[0]):
        at = pl.ds(c * chunk, chunk)
        copies.append(pltpu.make_async_copy(flat_ref.at[:, at], flat_vmem.at[:, at], sems.at[c]))
        copies[c].start()
    nmodes, levels = z_ref.shape
    f32, bf16 = jnp.float32, jnp.bfloat16

    part = nmodes // 2
    z_ref[pl.ds(pl.multiple_of(part * core_ref[0], 8), part), :] = mine_ref[...]
    z_ref[pl.ds(pl.multiple_of(part * (1 - core_ref[0]), 8), part), :] = other_ref[...]
    z = z_ref[...]
    gram = dot(z, z, ((1,), (1,)))
    padded = jnp.concatenate([gram, jnp.zeros((nmodes, LANES - nmodes), f32)], axis=1)
    inverse_cholesky(padded, linv_ref)
    basis = dot(linv_ref[:, :nmodes], z)
    basis_ref[...] = basis
    modes_by_hours = spread(nmodes, hours, nmodes * hours, True)
    tall = dot(modes_by_hours, basis.astype(bf16), precision=None).astype(bf16)
    wide = dot(tall, spread(levels, hours, total), precision=None)
    weight_ref[...] = jnp.where(same(*wide.shape, lambda i: lax.rem(i, hours)), wide, 0.0).astype(bf16)

    groups, _, rows, _ = out_ref.shape
    for c, copy in enumerate(copies):
        copy.wait()
        made = dot(weight_ref[...], flat_vmem[:, c * chunk : (c + 1) * chunk], precision=None)
        for a in range(groups):
            for b in range(chunk // LANES):
                out_ref[a, c * chunk // LANES + b] = made[rows * a : rows * (a + 1), LANES * b : LANES * (b + 1)].astype(bf16)


def project(core, mine, other, flat, hours, groups):
    total, columns = flat.shape
    part, levels = mine.shape
    nmodes = 2 * part
    rows = hours * nmodes // groups
    smem, vm = pl.BlockSpec(memory_space=pltpu.SMEM), pl.BlockSpec(memory_space=pltpu.VMEM)
    return pl.pallas_call(
        functools.partial(project_kernel, hours),
        out_shape=(
            jax.ShapeDtypeStruct((nmodes, levels), jnp.float32),
            jax.ShapeDtypeStruct((groups, columns // LANES, rows, LANES), jnp.bfloat16),
        ),
        in_specs=[smem, vm, vm, pl.BlockSpec(memory_space=pltpu.HBM)],
        out_specs=(vm, vm),
        scratch_shapes=[
            pltpu.VMEM((hours * nmodes, total), jnp.bfloat16),
            pltpu.VMEM((nmodes, LANES), jnp.float32),
            pltpu.VMEM((nmodes, levels), jnp.float32),
            pltpu.VMEM((total, columns), jnp.bfloat16),
            pltpu.SemaphoreType.DMA((4,)),
        ],
        compiler_params=pltpu.CompilerParams(vmem_limit_bytes=60 * 2**20),
        name="project",
    )(core, mine, other, flat)


def hour_gram_kernel(scale, core_ref, lag_ref, got_ref, out_ref, flat_ref, gram_ref, half_ref):
    senders, rows, _ = got_ref.shape
    width = half_ref.shape[0]
    f32, bf16 = jnp.float32, jnp.bfloat16
    hours = flat_ref.shape[0] // senders
    per = rows // hours
    many = 32
    size = many * rows
    new = counted((size, 1), 0)
    span = many * hours
    mode, rest = lax.div(new, span), lax.rem(new, span)
    wanted = lax.div(rest, hours) * rows + mode * hours + lax.rem(rest, hours)
    pick = jnp.where(counted((1, size), 1) == wanted, 1.0, 0.0).astype(bf16)
    for s in range(0, senders, 2 * many):
        pair = [got_ref[s + many * k : s + many * (k + 1)].reshape(size, LANES) for k in range(2)]
        moved = dot(pick, jnp.concatenate(pair, axis=1), precision=None).astype(bf16)
        for k in range(2):
            for m in range(per):
                flat_ref[hours * s + span * k : hours * s + span * (k + 1), LANES * m : LANES * (m + 1)] = moved[
                    span * m : span * (m + 1), LANES * k : LANES * (k + 1)
                ]
    for i in range(0, flat_ref.shape[0], 256):
        band = dot(flat_ref[i : i + 256, :], flat_ref[...], ((1,), (1,)), None)
        for b in range(gram_ref.shape[0]):
            gram_ref[b, i : i + 256, :] = band[:, LANES * b : LANES * (b + 1)]

    blocks, some = width // LANES, 32
    lane = lax.broadcasted_iota(jnp.int32, (some, LANES), 1)
    lags = [lag_ref[j] for j in range(lag_ref.shape[0])]
    whole = [lax.div(offset, LANES) for offset in lags]
    part = [lax.rem(offset, LANES) for offset in lags]
    for i in range(blocks):
        wanted = [(i + d) % blocks for d in range(4)]
        for r in range(LANES * i, LANES * (i + 1), some):
            acc = [jnp.zeros((some, LANES), f32)] * 4
            for j, offset in enumerate(lags):
                load = {}
                for b in sorted(set(wanted) | {w + 1 for w in wanted}):
                    block = gram_ref[jnp.minimum(whole[j] + b, gram_ref.shape[0] - 1), pl.ds(offset + r, some), :]
                    load[b] = pltpu.roll(block, lax.rem(LANES - part[j], LANES), 1)
                acc = [a + jnp.where(lane < LANES - part[j], load[w], load[w + 1]) for a, w in zip(acc, wanted)]
            for d in range(4):
                half_ref[r : r + some, LANES * d : LANES * (d + 1)] = acc[d] * scale
    _, each, high, _ = out_ref.shape
    for c in range(2):
        for k in range(each):
            at = (c * each + k) * high
            out_ref[lax.bitwise_xor(c, core_ref[0]), k] = half_ref[at : at + high, :]


def hour_gram(core, lags, got, width, hours, scale):
    senders, rows, _ = got.shape
    total = senders * hours
    wide = 4 * LANES
    smem, vm = pl.BlockSpec(memory_space=pltpu.SMEM), pl.BlockSpec(memory_space=pltpu.VMEM)
    return pl.pallas_call(
        functools.partial(hour_gram_kernel, scale),
        out_shape=jax.ShapeDtypeStruct((2, 16, width // 32, wide), jnp.float32),
        in_specs=[smem, smem, vm],
        out_specs=vm,
        scratch_shapes=[
            pltpu.VMEM((total, rows // hours * LANES), jnp.bfloat16),
            pltpu.VMEM((total // LANES, total, LANES), jnp.float32),
            pltpu.VMEM((width, wide), jnp.float32),
        ],
        compiler_params=pltpu.CompilerParams(vmem_limit_bytes=48 * 2**20),
        name="hour_gram",
    )(core, lags, got)


PLANE = ("y", "x")
COLUMN = ("zl", "zh")


def other_core(x):
    return lax.ppermute(x, "co", [(0, 1), (1, 0)])


def exchange(x, axes):
    return lax.all_to_all(x, axes, split_axis=0, concat_axis=0, tiled=True)


def collect(x, axes):
    return exchange(jnp.broadcast_to(x, (lax.axis_size(axes),) + x.shape), axes)


def sum_over(x, axes):
    return jnp.sum(collect(x, axes), axis=0)


def sum_pieces(pieces):
    here = pieces[0] + other_core(pieces[1])
    mine = jnp.sum(exchange(here, PLANE), axis=0)
    return collect(sum_over(mine, COLUMN), PLANE)


def body(field, level_start, time_start, lag_offsets):
    hour_count, levels, columns = field.shape
    devices = lax.axis_size(AXES)
    hours_all = hour_count * devices
    width = time_start.shape[0]
    nmodes = level_start.shape[1]
    core = lax.axis_index("co").reshape(1)
    scale = 1.0 / (hours_all * columns)
    halves, level_hours = level_product(core, jnp.transpose(field, (1, 0, 2)), level_start.T, scale)
    z = halves[0] + other_core(halves[1])
    z = sum_over(sum_over(z, PLANE), COLUMN)
    level_basis, sent = project(core, z, other_core(z), level_hours, hour_count, 8)
    sent = sent.reshape(devices, 24, LANES)
    received = exchange(sent, AXES)
    scale = 1.0 / (lag_offsets.shape[0] * nmodes * columns)
    summed = sum_pieces(hour_gram(core, lag_offsets, received, width, hour_count, scale))
    low_rank = truncate(core, summed, other_core(summed), time_start)
    return (level_basis.T, low_rank)


def solution(mesh):
    fine = Mesh(mesh.devices.reshape(SIZES), AXES)
    return jax.shard_map(
        body,
        mesh=fine,
        in_specs=(P(AXES, None, None), P(), P(), P()),
        out_specs=(P(), P()),
        check_vma=False,
    )
```

```python
import functools
import jax
import jax.numpy as jnp
from jax import lax
from jax.experimental import pallas as pl
from jax.experimental.pallas import tpu as pltpu
from jax.sharding import Mesh, PartitionSpec as P

AXES = ("zl", "co", "y", "zh", "x")
SIZES = (2, 2, 4, 4, 4)
HIGH = lax.Precision.HIGHEST
LANES = 128
ITERS = 3

def dot(a, b, dims=((1,), (0,)), precision=HIGH):
    return lax.dot_general(a, b, (dims, ((), ())), precision=precision, preferred_element_type=jnp.float32)


def split(x):
    hi = x.astype(jnp.bfloat16)
    rest = x - hi.astype(jnp.float32)
    mid = rest.astype(jnp.bfloat16)
    low = (rest - mid.astype(jnp.float32)).astype(jnp.bfloat16)
    return hi, mid, low


def across(row):
    return jnp.broadcast_to(row, (8, LANES))


def inverse_cholesky(gram, out_ref):
    n = gram.shape[0]
    tiles = n // 8
    lane = lax.broadcasted_iota(jnp.int32, (8, LANES), 1)
    sub = lax.broadcasted_iota(jnp.int32, (8, LANES), 0)
    left = [gram[8 * t : 8 * t + 8, :] for t in range(tiles)]
    right = [jnp.where(lane == sub + 8 * t, 1.0, 0.0) for t in range(tiles)]
    for here in range(tiles):
        cols = [
            {
                t: jnp.broadcast_to(left[t][:, 8 * here + k : 8 * here + k + 1], (8, LANES))
                for t in range(here, tiles)
            }
            for k in range(8)
        ]
        entry = {(r, k): across(cols[k][here][r : r + 1, :]) for k in range(8) for r in range(k, 8)}
        low, inv = {}, []
        for k in range(8):
            inv.append(lax.rsqrt(entry[k, k]))
            for r in range(k + 1, 8):
                low[r, k] = entry[r, k] * inv[k]
            for q in range(k + 1, 8):
                for r in range(q, 8):
                    entry[r, q] = entry[r, q] - low[r, k] * low[q, k]
        side = [across(left[here][k : k + 1, :]) for k in range(8)], [across(right[here][k : k + 1, :]) for k in range(8)]
        for k in range(8):
            for row in side:
                row[k] = row[k] * inv[k]
                for r in range(k + 1, 8):
                    row[r] = row[r] - low[r, k] * row[k]
            out_ref[8 * here + k : 8 * here + k + 1, :] = side[1][k][0:1, :]
        for t in range(here + 1, tiles):
            mult = [cols[k][t] for k in range(8)]
            for k in range(8):
                mult[k] = mult[k] * inv[k]
                for r in range(k + 1, 8):
                    mult[r] = mult[r] - mult[k] * low[r, k]
                left[t] = left[t] - mult[k] * side[0][k]
                right[t] = right[t] - mult[k] * side[1][k]


def truncate_kernel(core_ref, mine_ref, other_ref, start_ref, out_ref, d_ref, half_ref, split_ref, z_ref, w_ref, linv_ref, sems):
    each, high, _ = mine_ref.shape
    width = d_ref.shape[0]
    for ref, core in ((mine_ref, core_ref[0]), (other_ref, 1 - core_ref[0])):
        for k in range(each):
            half_ref[pl.ds(pl.multiple_of((core * each + k) * high, 8), high), :] = ref[k]
    for (down, along), (i, j) in stored(width // LANES):
        block = half_ref[LANES * down : LANES * (down + 1), LANES * along : LANES * (along + 1)]
        d_ref[LANES * i : LANES * (i + 1), LANES * j : LANES * (j + 1)] = block
        if i != j:
            d_ref[LANES * j : LANES * (j + 1), LANES * i : LANES * (i + 1)] = block.T
    lagged = d_ref[...]
    rows = jnp.sum(lagged, axis=1, keepdims=True) * (1.0 / width)
    cols = jnp.sum(lagged, axis=0, keepdims=True) * (1.0 / width)
    mean = jnp.sum(rows, axis=0, keepdims=True) * (1.0 / width)
    debiased = lagged - rows - cols + mean
    for k, part in enumerate(split(debiased)):
        split_ref[k] = part

    def times(x):
        n = x.shape[0]
        parts = jnp.concatenate(split(x), axis=0)
        by = lambda m, k: dot(parts[: m * n], split_ref[k], precision=None)
        one, two, three = by(3, 0), by(2, 1), by(1, 2)
        small = one[2 * n :] + two[n:] + three
        return one[:n] + ((one[n : 2 * n] + two[:n]) + small)

    z_ref[...] = times(start_ref[...].T)

    def step(_, carry):
        z = z_ref[...]
        inverse_cholesky(dot(z, z, ((1,), (1,))), linv_ref)
        w_ref[...] = times(z)
        @pl.when(_ < ITERS - 1)
        def _more():
            z_ref[...] = dot(linv_ref[...], w_ref[...])
        return carry

    lax.fori_loop(0, ITERS, step, 0)
    linv = linv_ref[...]
    basis = dot(linv, z_ref[...])
    inner = dot(dot(linv, w_ref[...]), basis, ((1,), (1,)))
    spanned = dot(inner, basis)
    copies = []
    for r in range(sems.shape[0]):
        at = pl.ds(r * width // sems.shape[0], width // sems.shape[0])
        rows = basis[:, r * width // sems.shape[0] : (r + 1) * width // sems.shape[0]]
        d_ref[at, :] = dot(rows, spanned, ((0,), (0,)), lax.Precision.HIGH)
        copies.append(pltpu.make_async_copy(d_ref.at[at, :], out_ref.at[at, :], sems.at[r]))
        copies[r].start()
    for copy in copies:
        copy.wait()


def truncate(core, mine, other, start):
    width, rank = start.shape
    f32 = jnp.float32
    vm = pl.BlockSpec(memory_space=pltpu.VMEM)
    return pl.pallas_call(
        truncate_kernel,
        out_shape=jax.ShapeDtypeStruct((width, width), f32),
        in_specs=[pl.BlockSpec(memory_space=pltpu.SMEM), vm, vm, vm],
        out_specs=pl.BlockSpec(memory_space=pltpu.HBM),
        scratch_shapes=[
            pltpu.VMEM((width, width), f32),
            pltpu.VMEM((width, 4 * LANES), f32),
            pltpu.VMEM((3, width, width), jnp.bfloat16),
            pltpu.VMEM((rank, width), f32),
            pltpu.VMEM((rank, width), f32),
            pltpu.VMEM((rank, rank), f32),
            pltpu.SemaphoreType.DMA((3,)),
        ],
        compiler_params=pltpu.CompilerParams(vmem_limit_bytes=48 * 2**20),
        name="truncate",
    )(core, mine, other, start)


def counted(shape, axis):
    return lax.broadcasted_iota(jnp.int32, shape, axis)


def spread(levels, hours, places, turned=False):
    if turned:
        place, level = counted((places, 1), 0), counted((1, levels), 1)
    else:
        place, level = counted((1, places), 1), counted((levels, 1), 0)
    first = level * hours
    return jnp.where((place >= first) & (place < first + hours), 1.0, 0.0).astype(jnp.bfloat16)


def same(rows, columns, of):
    return of(counted((rows, 1), 0)) == of(counted((1, columns), 1))


def level_gram_kernel(scale, core_ref, field_ref, start_ref, mine_ref, other_ref, flat_ref, acc_ref, field_vmem, flat_vmem, sems, flat_sems):
    levels, hours, columns = field_ref.shape
    total = flat_ref.shape[0]
    chunk = columns // sems.shape[0]
    tile = 256
    copies, writes = [], []
    for c in range(sems.shape[0]):
        at = pl.ds(c * chunk, chunk)
        copies.append(pltpu.make_async_copy(field_ref.at[:, :, at], field_vmem.at[:, :, at], sems.at[c]))
        copies[c].start()
    for c, copy in enumerate(copies):
        copy.wait()
        flat = field_vmem[:, :, c * chunk : (c + 1) * chunk].reshape(levels * hours, chunk)
        flat = jnp.concatenate([flat, jnp.zeros((total - levels * hours, chunk), jnp.bfloat16)], axis=0)
        at = pl.ds(c * chunk, chunk)
        flat_vmem[:, at] = flat
        writes.append(pltpu.make_async_copy(flat_vmem.at[:, at], flat_ref.at[:, at], flat_sems.at[c]))
        writes[c].start()
        for j in range(0, total, tile):
            wide = min(tile, total - j)
            block = dot(flat[j:], flat[j : j + wide], ((1,), (1,)), None)
            acc_ref[j:, j : j + wide] = block if c == 0 else acc_ref[j:, j : j + wide] + block
    left = spread(levels, hours, total)
    right = spread(levels, hours, total, True)
    over = []
    for j in range(0, total, tile):
        wide = min(tile, total - j)
        row, col = counted((total - j, 1), 0), counted((1, wide), 1)
        weight = jnp.where(lax.rem(row, hours) == lax.rem(col, hours), jnp.where(row < wide, 0.5, 1.0), 0.0)
        half = acc_ref[j:, j : j + wide] * weight
        over.append(sum(dot(left[:, j:], part, precision=None) for part in reversed(split(half))))
    over = jnp.concatenate(over, axis=1)
    gram = sum(dot(part, right, precision=None) for part in reversed(split(over)))
    z = (dot(start_ref[...], gram) + dot(start_ref[...], gram, ((1,), (1,)))) * scale
    part = z.shape[0] // 2
    first = core_ref[0] == 0
    mine_ref[...] = jnp.where(first, z[:part], z[part:])
    other_ref[...] = jnp.where(first, z[part:], z[:part])
    for write in writes:
        write.wait()


def level_product(core, field, start, scale):
    levels, hours, columns = field.shape
    nmodes = start.shape[0]
    total = -(-levels * hours // 16) * 16
    smem, vm = pl.BlockSpec(memory_space=pltpu.SMEM), pl.BlockSpec(memory_space=pltpu.VMEM)
    return pl.pallas_call(
        functools.partial(level_gram_kernel, scale),
        out_shape=(
            jax.ShapeDtypeStruct((nmodes // 2, levels), jnp.float32),
            jax.ShapeDtypeStruct((nmodes // 2, levels), jnp.float32),
            jax.ShapeDtypeStruct((total, columns), jnp.bfloat16),
        ),
        in_specs=[smem, pl.BlockSpec(memory_space=pltpu.HBM), vm],
        out_specs=(vm, vm, pl.BlockSpec(memory_space=pltpu.HBM)),
        scratch_shapes=[
            pltpu.VMEM((total, total), jnp.float32),
            pltpu.VMEM((levels, hours, columns), jnp.bfloat16),
            pltpu.VMEM((total, columns), jnp.bfloat16),
            pltpu.SemaphoreType.DMA((4,)),
            pltpu.SemaphoreType.DMA((4,)),
        ],
        compiler_params=pltpu.CompilerParams(vmem_limit_bytes=58 * 2**20),
        name="level_product",
    )(core, field, start)


def project_kernel(hours, core_ref, mine_ref, other_ref, flat_ref, basis_ref, out_ref, weight_ref, linv_ref, z_ref, flat_vmem, sems):
    total, columns = flat_ref.shape
    chunk = columns // sems.shape[0]
    copies = []
    for c in range(sems.shape[0]):
        at = pl.ds(c * chunk, chunk)
        copies.append(pltpu.make_async_copy(flat_ref.at[:, at], flat_vmem.at[:, at], sems.at[c]))
        copies[c].start()
    nmodes, levels = z_ref.shape
    f32, bf16 = jnp.float32, jnp.bfloat16

    part = nmodes // 2
    z_ref[pl.ds(pl.multiple_of(part * core_ref[0], 8), part), :] = mine_ref[...]
    z_ref[pl.ds(pl.multiple_of(part * (1 - core_ref[0]), 8), part), :] = other_ref[...]
    z = z_ref[...]
    gram = dot(z, z, ((1,), (1,)))
    padded = jnp.concatenate([gram, jnp.zeros((nmodes, LANES - nmodes), f32)], axis=1)
    inverse_cholesky(padded, linv_ref)
    basis = dot(linv_ref[:, :nmodes], z)
    basis_ref[...] = basis
    modes_by_hours = spread(nmodes, hours, nmodes * hours, True)
    tall = dot(modes_by_hours, basis.astype(bf16), precision=None).astype(bf16)
    wide = dot(tall, spread(levels, hours, total), precision=None)
    weight_ref[...] = jnp.where(same(*wide.shape, lambda i: lax.rem(i, hours)), wide, 0.0).astype(bf16)

    groups, _, rows, _ = out_ref.shape
    for c, copy in enumerate(copies):
        copy.wait()
        made = dot(weight_ref[...], flat_vmem[:, c * chunk : (c + 1) * chunk], precision=None)
        for a in range(groups):
            for b in range(chunk // LANES):
                out_ref[a, c * chunk // LANES + b] = made[rows * a : rows * (a + 1), LANES * b : LANES * (b + 1)].astype(bf16)


def project(core, mine, other, flat, hours, groups):
    total, columns = flat.shape
    part, levels = mine.shape
    nmodes = 2 * part
    rows = hours * nmodes // groups
    smem, vm = pl.BlockSpec(memory_space=pltpu.SMEM), pl.BlockSpec(memory_space=pltpu.VMEM)
    return pl.pallas_call(
        functools.partial(project_kernel, hours),
        out_shape=(
            jax.ShapeDtypeStruct((nmodes, levels), jnp.float32),
            jax.ShapeDtypeStruct((groups, columns // LANES, rows, LANES), jnp.bfloat16),
        ),
        in_specs=[smem, vm, vm, pl.BlockSpec(memory_space=pltpu.HBM)],
        out_specs=(vm, vm),
        scratch_shapes=[
            pltpu.VMEM((hours * nmodes, total), jnp.bfloat16),
            pltpu.VMEM((nmodes, LANES), jnp.float32),
            pltpu.VMEM((nmodes, levels), jnp.float32),
            pltpu.VMEM((total, columns), jnp.bfloat16),
            pltpu.SemaphoreType.DMA((4,)),
        ],
        compiler_params=pltpu.CompilerParams(vmem_limit_bytes=58 * 2**20),
        name="project",
    )(core, mine, other, flat)


def stored(blocks):
    pairs = [((i, j - i), (i, j)) for i in range(blocks) for j in range(i, min(i + 4, blocks))]
    return pairs + [((3, 3), (0, 4)), ((4, 2), (0, 5)), ((4, 3), (1, 5))]


def hour_gram_kernel(scale, core_ref, lag_ref, got_ref, out_ref, flat_ref, gram_ref, half_ref):
    senders, rows, _ = got_ref.shape
    width = half_ref.shape[0]
    f32, bf16 = jnp.float32, jnp.bfloat16
    hours = flat_ref.shape[0] // senders
    per = rows // hours
    many = 32
    size = many * rows
    new = counted((size, 1), 0)
    span = many * hours
    mode, rest = lax.div(new, span), lax.rem(new, span)
    wanted = lax.div(rest, hours) * rows + mode * hours + lax.rem(rest, hours)
    pick = jnp.where(counted((1, size), 1) == wanted, 1.0, 0.0).astype(bf16)
    for s in range(0, senders, 2 * many):
        pair = [got_ref[s + many * k : s + many * (k + 1)].reshape(size, LANES) for k in range(2)]
        moved = dot(pick, jnp.concatenate(pair, axis=1), precision=None).astype(bf16)
        for k in range(2):
            for m in range(per):
                flat_ref[hours * s + span * k : hours * s + span * (k + 1), LANES * m : LANES * (m + 1)] = moved[
                    span * m : span * (m + 1), LANES * k : LANES * (k + 1)
                ]
    for i in range(0, flat_ref.shape[0], 256):
        first = max(i - LANES, 0)
        band = dot(flat_ref[i : i + 256, :], flat_ref[first:, :], ((1,), (1,)), None)
        for b in range(first // LANES, gram_ref.shape[0]):
            gram_ref[b, i : i + 256, :] = band[:, LANES * b - first : LANES * (b + 1) - first]

    blocks, some = width // LANES, 32
    lane = lax.broadcasted_iota(jnp.int32, (some, LANES), 1)
    lags = [lag_ref[j] for j in range(lag_ref.shape[0])]
    whole = [lax.div(offset, LANES) for offset in lags]
    part = [lax.rem(offset, LANES) for offset in lags]
    spots = {pair: spot for spot, pair in stored(blocks)}
    for i in range(blocks):
        for r in range(0, LANES, some):
            acc = {b: jnp.zeros((some, LANES), f32) for b in range(i, blocks)}
            for j, offset in enumerate(lags):
                load = {}
                for b in range(i, blocks + 1):
                    column = jnp.minimum(whole[j] + b, gram_ref.shape[0] - 1)
                    block = gram_ref[column, pl.ds(offset + LANES * i + r, some), :]
                    load[b] = pltpu.roll(block, lax.rem(LANES - part[j], LANES), 1)
                acc = {b: acc[b] + jnp.where(lane < LANES - part[j], load[b], load[b + 1]) for b in acc}
            for b in acc:
                down, along = spots[i, b]
                half_ref[LANES * down + r : LANES * down + r + some, LANES * along : LANES * (along + 1)] = acc[b] * scale
    half_ref[width - LANES :, LANES:] = jnp.zeros((LANES, half_ref.shape[1] - LANES), f32)
    _, each, high, _ = out_ref.shape
    for c in range(2):
        for k in range(each):
            at = (c * each + k) * high
            out_ref[lax.bitwise_xor(c, core_ref[0]), k] = half_ref[at : at + high, :]


def hour_gram(core, lags, got, width, hours, scale):
    senders, rows, _ = got.shape
    total = senders * hours
    wide = 4 * LANES
    smem, vm = pl.BlockSpec(memory_space=pltpu.SMEM), pl.BlockSpec(memory_space=pltpu.VMEM)
    return pl.pallas_call(
        functools.partial(hour_gram_kernel, scale),
        out_shape=jax.ShapeDtypeStruct((2, 16, width // 32, wide), jnp.float32),
        in_specs=[smem, smem, vm],
        out_specs=vm,
        scratch_shapes=[
            pltpu.VMEM((total, rows // hours * LANES), jnp.bfloat16),
            pltpu.VMEM((total // LANES, total, LANES), jnp.float32),
            pltpu.VMEM((width, wide), jnp.float32),
        ],
        compiler_params=pltpu.CompilerParams(vmem_limit_bytes=48 * 2**20),
        name="hour_gram",
    )(core, lags, got)


PLANE = ("y", "x")
COLUMN = ("zl", "zh")


def other_core(x):
    return lax.ppermute(x, "co", [(0, 1), (1, 0)])


def exchange(x, axes):
    return lax.all_to_all(x, axes, split_axis=0, concat_axis=0, tiled=True)


def collect(x, axes):
    return exchange(jnp.broadcast_to(x, (lax.axis_size(axes),) + x.shape), axes)


def sum_over(x, axes):
    return jnp.sum(collect(x, axes), axis=0)


def sum_pieces(pieces):
    here = pieces[0] + other_core(pieces[1])
    mine = jnp.sum(exchange(here, PLANE), axis=0)
    return collect(sum_over(mine, COLUMN), PLANE)


def body(field, level_start, time_start, lag_offsets):
    hour_count, levels, columns = field.shape
    devices = lax.axis_size(AXES)
    hours_all = hour_count * devices
    width = time_start.shape[0]
    nmodes = level_start.shape[1]
    core = lax.axis_index("co").reshape(1)
    scale = 1.0 / (hours_all * columns)
    z, other, level_hours = level_product(core, jnp.transpose(field, (1, 0, 2)), level_start.T, scale)
    z = z + other_core(other)
    z = sum_over(sum_over(z, PLANE), COLUMN)
    level_basis, sent = project(core, z, other_core(z), level_hours, hour_count, 8)
    sent = sent.reshape(devices, 24, LANES)
    received = exchange(sent, AXES)
    scale = 1.0 / (lag_offsets.shape[0] * nmodes * columns)
    summed = sum_pieces(hour_gram(core, lag_offsets, received, width, hour_count, scale))
    low_rank = truncate(core, summed, other_core(summed), time_start)
    return (level_basis.T, low_rank)


def solution(mesh):
    fine = Mesh(mesh.devices.reshape(SIZES), AXES)
    return jax.shard_map(
        body,
        mesh=fine,
        in_specs=(P(AXES, None, None), P(), P(), P()),
        out_specs=(P(), P()),
        check_vma=False,
    )
```

```python
import functools
import jax
import jax.numpy as jnp
from jax import lax
from jax.experimental import pallas as pl
from jax.experimental.pallas import tpu as pltpu
from jax.sharding import Mesh, PartitionSpec as P

AXES = ("zl", "co", "y", "zh", "x")
SIZES = (2, 2, 4, 4, 4)
HIGH = lax.Precision.HIGHEST
LANES = 128
ITERS = 3

def dot(a, b, dims=((1,), (0,)), precision=HIGH):
    return lax.dot_general(a, b, (dims, ((), ())), precision=precision, preferred_element_type=jnp.float32)


def split(x):
    hi = x.astype(jnp.bfloat16)
    rest = x - hi.astype(jnp.float32)
    mid = rest.astype(jnp.bfloat16)
    low = (rest - mid.astype(jnp.float32)).astype(jnp.bfloat16)
    return hi, mid, low


def across(row):
    return jnp.broadcast_to(row, (8, LANES))


def inverse_cholesky(gram, out_ref):
    n = gram.shape[0]
    tiles = n // 8
    lane = lax.broadcasted_iota(jnp.int32, (8, LANES), 1)
    sub = lax.broadcasted_iota(jnp.int32, (8, LANES), 0)
    left = [gram[8 * t : 8 * t + 8, :] for t in range(tiles)]
    right = [jnp.where(lane == sub + 8 * t, 1.0, 0.0) for t in range(tiles)]
    for here in range(tiles):
        cols = [
            {
                t: jnp.broadcast_to(left[t][:, 8 * here + k : 8 * here + k + 1], (8, LANES))
                for t in range(here, tiles)
            }
            for k in range(8)
        ]
        entry = {(r, k): across(cols[k][here][r : r + 1, :]) for k in range(8) for r in range(k, 8)}
        low, inv = {}, []
        for k in range(8):
            inv.append(lax.rsqrt(entry[k, k]))
            for r in range(k + 1, 8):
                low[r, k] = entry[r, k] * inv[k]
            for q in range(k + 1, 8):
                for r in range(q, 8):
                    entry[r, q] = entry[r, q] - low[r, k] * low[q, k]
        side = [across(left[here][k : k + 1, :]) for k in range(8)], [across(right[here][k : k + 1, :]) for k in range(8)]
        for k in range(8):
            for row in side:
                row[k] = row[k] * inv[k]
                for r in range(k + 1, 8):
                    row[r] = row[r] - low[r, k] * row[k]
            out_ref[8 * here + k : 8 * here + k + 1, :] = side[1][k][0:1, :]
        back = list(side[0]), list(side[1])
        for row in back:
            for k in reversed(range(8)):
                row[k] = row[k] * inv[k]
                for r in range(k):
                    row[r] = row[r] - low[k, r] * row[k]
        for t in range(here + 2, tiles):
            for k in range(8):
                left[t] = left[t] - cols[k][t] * back[0][k]
                right[t] = right[t] - cols[k][t] * back[1][k]
        for t in range(here + 1, min(here + 2, tiles)):
            mult = [cols[k][t] for k in range(8)]
            for k in range(8):
                mult[k] = mult[k] * inv[k]
                for r in range(k + 1, 8):
                    mult[r] = mult[r] - mult[k] * low[r, k]
                left[t] = left[t] - mult[k] * side[0][k]
                right[t] = right[t] - mult[k] * side[1][k]


def truncate_kernel(core_ref, mine_ref, other_ref, start_ref, out_ref, d_ref, half_ref, split_ref, z_ref, w_ref, linv_ref, sems):
    each, high, _ = mine_ref.shape
    width = d_ref.shape[0]
    for ref, core in ((mine_ref, core_ref[0]), (other_ref, 1 - core_ref[0])):
        for k in range(each):
            half_ref[pl.ds(pl.multiple_of((core * each + k) * high, 8), high), :] = ref[k]
    for spot, (i, j) in enumerate(upper(width // LANES)):
        block = half_ref[LANES * spot : LANES * (spot + 1), :]
        d_ref[LANES * i : LANES * (i + 1), LANES * j : LANES * (j + 1)] = block
        if i != j:
            d_ref[LANES * j : LANES * (j + 1), LANES * i : LANES * (i + 1)] = block.T
    lagged = d_ref[...]
    rows = jnp.sum(lagged, axis=1, keepdims=True) * (1.0 / width)
    cols = jnp.sum(lagged, axis=0, keepdims=True) * (1.0 / width)
    mean = jnp.sum(rows, axis=0, keepdims=True) * (1.0 / width)
    debiased = lagged - rows - cols + mean
    for k, part in enumerate(split(debiased)):
        split_ref[k] = part

    def times(x):
        n = x.shape[0]
        parts = jnp.concatenate(split(x), axis=0)
        by = lambda m, k: dot(parts[: m * n], split_ref[k], precision=None)
        one, two, three = by(3, 0), by(2, 1), by(1, 2)
        small = one[2 * n :] + two[n:] + three
        return one[:n] + ((one[n : 2 * n] + two[:n]) + small)

    z_ref[...] = times(start_ref[...].T)

    def step(_, carry):
        z = z_ref[...]
        inverse_cholesky(dot(z, z, ((1,), (1,))), linv_ref)
        w_ref[...] = times(z)
        @pl.when(_ < ITERS - 1)
        def _more():
            z_ref[...] = dot(linv_ref[...], w_ref[...])
        return carry

    lax.fori_loop(0, ITERS, step, 0)
    linv = linv_ref[...]
    basis = dot(linv, z_ref[...])
    inner = dot(dot(linv, w_ref[...]), basis, ((1,), (1,)))
    spanned = dot(inner, basis)
    copies = []
    for r in range(sems.shape[0]):
        at = pl.ds(r * width // sems.shape[0], width // sems.shape[0])
        rows = basis[:, r * width // sems.shape[0] : (r + 1) * width // sems.shape[0]]
        d_ref[at, :] = dot(rows, spanned, ((0,), (0,)), lax.Precision.HIGH)
        copies.append(pltpu.make_async_copy(d_ref.at[at, :], out_ref.at[at, :], sems.at[r]))
        copies[r].start()
    for copy in copies:
        copy.wait()


def truncate(core, mine, other, start):
    width, rank = start.shape
    f32 = jnp.float32
    vm = pl.BlockSpec(memory_space=pltpu.VMEM)
    return pl.pallas_call(
        truncate_kernel,
        out_shape=jax.ShapeDtypeStruct((width, width), f32),
        in_specs=[pl.BlockSpec(memory_space=pltpu.SMEM), vm, vm, vm],
        out_specs=pl.BlockSpec(memory_space=pltpu.HBM),
        scratch_shapes=[
            pltpu.VMEM((width, width), f32),
            pltpu.VMEM((mine.size // LANES * 2, LANES), f32),
            pltpu.VMEM((3, width, width), jnp.bfloat16),
            pltpu.VMEM((rank, width), f32),
            pltpu.VMEM((rank, width), f32),
            pltpu.VMEM((rank, rank), f32),
            pltpu.SemaphoreType.DMA((3,)),
        ],
        compiler_params=pltpu.CompilerParams(vmem_limit_bytes=48 * 2**20),
        name="truncate",
    )(core, mine, other, start)


def counted(shape, axis):
    return lax.broadcasted_iota(jnp.int32, shape, axis)


def spread(levels, hours, places, turned=False):
    if turned:
        place, level = counted((places, 1), 0), counted((1, levels), 1)
    else:
        place, level = counted((1, places), 1), counted((levels, 1), 0)
    first = level * hours
    return jnp.where((place >= first) & (place < first + hours), 1.0, 0.0).astype(jnp.bfloat16)


def same(rows, columns, of):
    return of(counted((rows, 1), 0)) == of(counted((1, columns), 1))


def level_gram_kernel(scale, core_ref, field_ref, start_ref, mine_ref, other_ref, flat_ref, acc_ref, field_vmem, flat_vmem, sems, flat_sems):
    levels, hours, columns = field_ref.shape
    total = flat_ref.shape[0]
    chunk = columns // sems.shape[0]
    tile = 256
    copies, writes = [], []
    for c in range(sems.shape[0]):
        at = pl.ds(c * chunk, chunk)
        copies.append(pltpu.make_async_copy(field_ref.at[:, :, at], field_vmem.at[:, :, at], sems.at[c]))
        copies[c].start()
    for c, copy in enumerate(copies):
        copy.wait()
        flat = field_vmem[:, :, c * chunk : (c + 1) * chunk].reshape(levels * hours, chunk)
        flat = jnp.concatenate([flat, jnp.zeros((total - levels * hours, chunk), jnp.bfloat16)], axis=0)
        at = pl.ds(c * chunk, chunk)
        flat_vmem[:, at] = flat
        writes.append(pltpu.make_async_copy(flat_vmem.at[:, at], flat_ref.at[:, at], flat_sems.at[c]))
        writes[c].start()
        for j in range(0, total, tile):
            wide = min(tile, total - j)
            block = dot(flat[j:], flat[j : j + wide], ((1,), (1,)), None)
            acc_ref[j:, j : j + wide] = block if c == 0 else acc_ref[j:, j : j + wide] + block
    left = spread(levels, hours, total)
    right = spread(levels, hours, total, True)
    over = []
    for j in range(0, total, tile):
        wide = min(tile, total - j)
        row, col = counted((total - j, 1), 0), counted((1, wide), 1)
        weight = jnp.where(lax.rem(row, hours) == lax.rem(col, hours), jnp.where(row < wide, 0.5, 1.0), 0.0)
        half = acc_ref[j:, j : j + wide] * weight
        over.append(sum(dot(left[:, j:], part, precision=None) for part in reversed(split(half))))
    over = jnp.concatenate(over, axis=1)
    gram = sum(dot(part, right, precision=None) for part in reversed(split(over)))
    z = (dot(start_ref[...], gram) + dot(start_ref[...], gram, ((1,), (1,)))) * scale
    part = z.shape[0] // 2
    first = core_ref[0] == 0
    mine_ref[...] = jnp.where(first, z[:part], z[part:])
    other_ref[...] = jnp.where(first, z[part:], z[:part])
    for write in writes:
        write.wait()


def level_product(core, field, start, scale):
    levels, hours, columns = field.shape
    nmodes = start.shape[0]
    total = -(-levels * hours // 16) * 16
    smem, vm = pl.BlockSpec(memory_space=pltpu.SMEM), pl.BlockSpec(memory_space=pltpu.VMEM)
    return pl.pallas_call(
        functools.partial(level_gram_kernel, scale),
        out_shape=(
            jax.ShapeDtypeStruct((nmodes // 2, levels), jnp.float32),
            jax.ShapeDtypeStruct((nmodes // 2, levels), jnp.float32),
            jax.ShapeDtypeStruct((total, columns), jnp.bfloat16),
        ),
        in_specs=[smem, pl.BlockSpec(memory_space=pltpu.HBM), vm],
        out_specs=(vm, vm, pl.BlockSpec(memory_space=pltpu.HBM)),
        scratch_shapes=[
            pltpu.VMEM((total, total), jnp.float32),
            pltpu.VMEM((levels, hours, columns), jnp.bfloat16),
            pltpu.VMEM((total, columns), jnp.bfloat16),
            pltpu.SemaphoreType.DMA((4,)),
            pltpu.SemaphoreType.DMA((4,)),
        ],
        compiler_params=pltpu.CompilerParams(vmem_limit_bytes=58 * 2**20),
        name="level_product",
    )(core, field, start)


def project_kernel(hours, core_ref, mine_ref, other_ref, flat_ref, basis_ref, out_ref, weight_ref, linv_ref, z_ref, flat_vmem, sems):
    total, columns = flat_ref.shape
    chunk = columns // sems.shape[0]
    copies = []
    for c in range(sems.shape[0]):
        at = pl.ds(c * chunk, chunk)
        copies.append(pltpu.make_async_copy(flat_ref.at[:, at], flat_vmem.at[:, at], sems.at[c]))
        copies[c].start()
    nmodes, levels = z_ref.shape
    f32, bf16 = jnp.float32, jnp.bfloat16

    part = nmodes // 2
    z_ref[pl.ds(pl.multiple_of(part * core_ref[0], 8), part), :] = mine_ref[...]
    z_ref[pl.ds(pl.multiple_of(part * (1 - core_ref[0]), 8), part), :] = other_ref[...]
    z = z_ref[...]
    gram = dot(z, z, ((1,), (1,)))
    padded = jnp.concatenate([gram, jnp.zeros((nmodes, LANES - nmodes), f32)], axis=1)
    inverse_cholesky(padded, linv_ref)
    basis = dot(linv_ref[:, :nmodes], z)
    basis_ref[...] = basis
    modes_by_hours = spread(nmodes, hours, nmodes * hours, True)
    tall = dot(modes_by_hours, basis.astype(bf16), precision=None).astype(bf16)
    wide = dot(tall, spread(levels, hours, total), precision=None)
    weight_ref[...] = jnp.where(same(*wide.shape, lambda i: lax.rem(i, hours)), wide, 0.0).astype(bf16)

    groups, _, rows, _ = out_ref.shape
    for c, copy in enumerate(copies):
        copy.wait()
        made = dot(weight_ref[...], flat_vmem[:, c * chunk : (c + 1) * chunk], precision=None)
        for a in range(groups):
            for b in range(chunk // LANES):
                out_ref[a, c * chunk // LANES + b] = made[rows * a : rows * (a + 1), LANES * b : LANES * (b + 1)].astype(bf16)


def project(core, mine, other, flat, hours, groups):
    total, columns = flat.shape
    part, levels = mine.shape
    nmodes = 2 * part
    rows = hours * nmodes // groups
    smem, vm = pl.BlockSpec(memory_space=pltpu.SMEM), pl.BlockSpec(memory_space=pltpu.VMEM)
    return pl.pallas_call(
        functools.partial(project_kernel, hours),
        out_shape=(
            jax.ShapeDtypeStruct((nmodes, levels), jnp.float32),
            jax.ShapeDtypeStruct((groups, columns // LANES, rows, LANES), jnp.bfloat16),
        ),
        in_specs=[smem, vm, vm, pl.BlockSpec(memory_space=pltpu.HBM)],
        out_specs=(vm, vm),
        scratch_shapes=[
            pltpu.VMEM((hours * nmodes, total), jnp.bfloat16),
            pltpu.VMEM((nmodes, LANES), jnp.float32),
            pltpu.VMEM((nmodes, levels), jnp.float32),
            pltpu.VMEM((total, columns), jnp.bfloat16),
            pltpu.SemaphoreType.DMA((4,)),
        ],
        compiler_params=pltpu.CompilerParams(vmem_limit_bytes=53 * 2**20),
        name="project",
    )(core, mine, other, flat)


def upper(blocks):
    return [(i, j) for i in range(blocks) for j in range(i, blocks)]


def piece_rows(blocks):
    return -(-len(upper(blocks)) * LANES // (32 * 8)) * 8


def hour_gram_kernel(scale, blocks, core_ref, lag_ref, got_ref, out_ref, flat_ref, gram_ref, half_ref):
    senders, rows, _ = got_ref.shape
    f32, bf16 = jnp.float32, jnp.bfloat16
    hours = flat_ref.shape[0] // senders
    per = rows // hours
    many = 32
    size = many * rows
    new = counted((size, 1), 0)
    span = many * hours
    mode, rest = lax.div(new, span), lax.rem(new, span)
    wanted = lax.div(rest, hours) * rows + mode * hours + lax.rem(rest, hours)
    pick = jnp.where(counted((1, size), 1) == wanted, 1.0, 0.0).astype(bf16)
    for s in range(0, senders, 2 * many):
        pair = [got_ref[s + many * k : s + many * (k + 1)].reshape(size, LANES) for k in range(2)]
        moved = dot(pick, jnp.concatenate(pair, axis=1), precision=None).astype(bf16)
        for k in range(2):
            for m in range(per):
                flat_ref[hours * s + span * k : hours * s + span * (k + 1), LANES * m : LANES * (m + 1)] = moved[
                    span * m : span * (m + 1), LANES * k : LANES * (k + 1)
                ]
    for i in range(0, flat_ref.shape[0], 256):
        first = max(i - LANES, 0)
        band = dot(flat_ref[i : i + 256, :], flat_ref[first:, :], ((1,), (1,)), None)
        for b in range(first // LANES, gram_ref.shape[0]):
            gram_ref[b, i : i + 256, :] = band[:, LANES * b - first : LANES * (b + 1) - first]

    some = 32
    lane = lax.broadcasted_iota(jnp.int32, (some, LANES), 1)
    lags = [lag_ref[j] for j in range(lag_ref.shape[0])]
    whole = [lax.div(offset, LANES) for offset in lags]
    part = [lax.rem(offset, LANES) for offset in lags]
    spots = {pair: spot for spot, pair in enumerate(upper(blocks))}
    for i in range(blocks):
        for r in range(0, LANES, some):
            acc = {b: jnp.zeros((some, LANES), f32) for b in range(i, blocks)}
            for j, offset in enumerate(lags):
                load = {}
                for b in range(i, blocks + 1):
                    column = jnp.minimum(whole[j] + b, gram_ref.shape[0] - 1)
                    block = gram_ref[column, pl.ds(offset + LANES * i + r, some), :]
                    load[b] = pltpu.roll(block, lax.rem(LANES - part[j], LANES), 1)
                acc = {b: acc[b] + jnp.where(lane < LANES - part[j], load[b], load[b + 1]) for b in acc}
            for b in acc:
                at = LANES * spots[i, b] + r
                half_ref[at : at + some, :] = acc[b] * scale
    made = LANES * len(spots)
    half_ref[made:, :] = jnp.zeros((half_ref.shape[0] - made, LANES), f32)
    _, each, high, _ = out_ref.shape
    for c in range(2):
        for k in range(each):
            at = (c * each + k) * high
            out_ref[lax.bitwise_xor(c, core_ref[0]), k] = half_ref[at : at + high, :]


def hour_gram(core, lags, got, width, hours, scale):
    senders, rows, _ = got.shape
    total = senders * hours
    blocks = width // LANES
    high = piece_rows(blocks)
    smem, vm = pl.BlockSpec(memory_space=pltpu.SMEM), pl.BlockSpec(memory_space=pltpu.VMEM)
    return pl.pallas_call(
        functools.partial(hour_gram_kernel, scale, blocks),
        out_shape=jax.ShapeDtypeStruct((2, 16, high, LANES), jnp.float32),
        in_specs=[smem, smem, vm],
        out_specs=vm,
        scratch_shapes=[
            pltpu.VMEM((total, rows // hours * LANES), jnp.bfloat16),
            pltpu.VMEM((total // LANES, total, LANES), jnp.float32),
            pltpu.VMEM((32 * high, LANES), jnp.float32),
        ],
        compiler_params=pltpu.CompilerParams(vmem_limit_bytes=48 * 2**20),
        name="hour_gram",
    )(core, lags, got)


PLANE = ("y", "x")
COLUMN = ("zl", "zh")


def other_core(x):
    return lax.ppermute(x, "co", [(0, 1), (1, 0)])


def exchange(x, axes):
    return lax.all_to_all(x, axes, split_axis=0, concat_axis=0, tiled=True)


def collect(x, axes):
    return exchange(jnp.broadcast_to(x, (lax.axis_size(axes),) + x.shape), axes)


def sum_over(x, axes):
    return jnp.sum(collect(x, axes), axis=0)


def sum_pieces(pieces):
    here = pieces[0] + other_core(pieces[1])
    mine = jnp.sum(exchange(here, PLANE), axis=0)
    return collect(sum_over(mine, COLUMN), PLANE)


def body(field, level_start, time_start, lag_offsets):
    hour_count, levels, columns = field.shape
    devices = lax.axis_size(AXES)
    hours_all = hour_count * devices
    width = time_start.shape[0]
    nmodes = level_start.shape[1]
    core = lax.axis_index("co").reshape(1)
    scale = 1.0 / (hours_all * columns)
    z, other, level_hours = level_product(core, jnp.transpose(field, (1, 0, 2)), level_start.T, scale)
    z = z + other_core(other)
    z = sum_over(sum_over(z, PLANE), COLUMN)
    level_basis, sent = project(core, z, other_core(z), level_hours, hour_count, 8)
    sent = sent.reshape(devices, 24, LANES)
    received = exchange(sent, AXES)
    scale = 1.0 / (lag_offsets.shape[0] * nmodes * columns)
    summed = sum_pieces(hour_gram(core, lag_offsets, received, width, hour_count, scale))
    low_rank = truncate(core, summed, other_core(summed), time_start)
    return (level_basis.T, low_rank)


def solution(mesh):
    fine = Mesh(mesh.devices.reshape(SIZES), AXES)
    return jax.shard_map(
        body,
        mesh=fine,
        in_specs=(P(AXES, None, None), P(), P(), P()),
        out_specs=(P(), P()),
        check_vma=False,
    )
```

```python
import functools
import jax
import jax.numpy as jnp
from jax import lax
from jax.experimental import pallas as pl
from jax.experimental.pallas import tpu as pltpu
from jax.sharding import Mesh, PartitionSpec as P

AXES = ("zl", "co", "y", "zh", "x")
SIZES = (2, 2, 4, 4, 4)
HIGH = lax.Precision.HIGHEST
LANES = 128
ITERS = 3

def dot(a, b, dims=((1,), (0,)), precision=HIGH):
    return lax.dot_general(a, b, (dims, ((), ())), precision=precision, preferred_element_type=jnp.float32)


def split(x):
    hi = x.astype(jnp.bfloat16)
    rest = x - hi.astype(jnp.float32)
    mid = rest.astype(jnp.bfloat16)
    low = (rest - mid.astype(jnp.float32)).astype(jnp.bfloat16)
    return hi, mid, low


def across(row):
    return jnp.broadcast_to(row, (8, LANES))


def inverse_cholesky(gram, out_ref):
    n = gram.shape[0]
    tiles = n // 8
    lane = lax.broadcasted_iota(jnp.int32, (8, LANES), 1)
    sub = lax.broadcasted_iota(jnp.int32, (8, LANES), 0)
    left = [gram[8 * t : 8 * t + 8, :] for t in range(tiles)]
    right = [jnp.where(lane == sub + 8 * t, 1.0, 0.0) for t in range(tiles)]
    for here in range(tiles):
        cols = [
            {
                t: jnp.broadcast_to(left[t][:, 8 * here + k : 8 * here + k + 1], (8, LANES))
                for t in range(here, tiles)
            }
            for k in range(8)
        ]
        entry = {(r, k): across(cols[k][here][r : r + 1, :]) for k in range(8) for r in range(k, 8)}
        low, inv = {}, []
        for k in range(8):
            inv.append(lax.rsqrt(entry[k, k]))
            for r in range(k + 1, 8):
                low[r, k] = entry[r, k] * inv[k]
            for q in range(k + 1, 8):
                for r in range(q, 8):
                    entry[r, q] = entry[r, q] - low[r, k] * low[q, k]
        side = [across(left[here][k : k + 1, :]) for k in range(8)], [across(right[here][k : k + 1, :]) for k in range(8)]
        for k in range(8):
            for row in side:
                row[k] = row[k] * inv[k]
                for r in range(k + 1, 8):
                    row[r] = row[r] - low[r, k] * row[k]
            out_ref[8 * here + k : 8 * here + k + 1, :] = side[1][k][0:1, :]
        back = list(side[0]), list(side[1])
        for row in back:
            for k in reversed(range(8)):
                row[k] = row[k] * inv[k]
                for r in range(k):
                    row[r] = row[r] - low[k, r] * row[k]
        for t in range(here + 2, tiles):
            for k in range(8):
                left[t] = left[t] - cols[k][t] * back[0][k]
                right[t] = right[t] - cols[k][t] * back[1][k]
        for t in range(here + 1, min(here + 2, tiles)):
            mult = [cols[k][t] for k in range(8)]
            for k in range(8):
                mult[k] = mult[k] * inv[k]
                for r in range(k + 1, 8):
                    mult[r] = mult[r] - mult[k] * low[r, k]
                left[t] = left[t] - mult[k] * side[0][k]
                right[t] = right[t] - mult[k] * side[1][k]


def truncate_kernel(core_ref, mine_ref, other_ref, start_ref, out_ref, d_ref, half_ref, split_ref, z_ref, w_ref, linv_ref, sems):
    each, high, _ = mine_ref.shape
    width = d_ref.shape[0]
    for ref, core in ((mine_ref, core_ref[0]), (other_ref, 1 - core_ref[0])):
        for k in range(each):
            half_ref[pl.ds(pl.multiple_of((core * each + k) * high, 8), high), :] = ref[k]
    for spot, (i, j) in enumerate(upper(width // LANES)):
        block = half_ref[LANES * spot : LANES * (spot + 1), :]
        d_ref[LANES * i : LANES * (i + 1), LANES * j : LANES * (j + 1)] = block
        if i != j:
            d_ref[LANES * j : LANES * (j + 1), LANES * i : LANES * (i + 1)] = block.T
    lagged = d_ref[...]
    rows = jnp.sum(lagged, axis=1, keepdims=True) * (1.0 / width)
    cols = jnp.sum(lagged, axis=0, keepdims=True) * (1.0 / width)
    mean = jnp.sum(rows, axis=0, keepdims=True) * (1.0 / width)
    debiased = lagged - rows - cols + mean
    for k, part in enumerate(split(debiased)):
        split_ref[k] = part

    def times(x):
        n = x.shape[0]
        parts = jnp.concatenate(split(x), axis=0)
        by = lambda m, k: dot(parts[: m * n], split_ref[k], precision=None)
        one, two, three = by(3, 0), by(2, 1), by(1, 2)
        small = one[2 * n :] + two[n:] + three
        return one[:n] + ((one[n : 2 * n] + two[:n]) + small)

    z_ref[...] = times(start_ref[...].T)

    def step(_, carry):
        z = z_ref[...]
        inverse_cholesky(dot(z, z, ((1,), (1,))), linv_ref)
        w_ref[...] = times(z)
        @pl.when(_ < ITERS - 1)
        def _more():
            z_ref[...] = dot(linv_ref[...], w_ref[...])
        return carry

    lax.fori_loop(0, ITERS, step, 0)
    linv = linv_ref[...]
    basis = dot(linv, z_ref[...])
    inner = dot(dot(linv, w_ref[...]), basis, ((1,), (1,)))
    spanned = dot(inner, basis)
    copies = []
    for r in range(sems.shape[0]):
        at = pl.ds(r * width // sems.shape[0], width // sems.shape[0])
        rows = basis[:, r * width // sems.shape[0] : (r + 1) * width // sems.shape[0]]
        d_ref[at, :] = dot(rows, spanned, ((0,), (0,)), lax.Precision.HIGH)
        copies.append(pltpu.make_async_copy(d_ref.at[at, :], out_ref.at[at, :], sems.at[r]))
        copies[r].start()
    for copy in copies:
        copy.wait()


def truncate(core, mine, other, start):
    width, rank = start.shape
    f32 = jnp.float32
    vm = pl.BlockSpec(memory_space=pltpu.VMEM)
    return pl.pallas_call(
        truncate_kernel,
        out_shape=jax.ShapeDtypeStruct((width, width), f32),
        in_specs=[pl.BlockSpec(memory_space=pltpu.SMEM), vm, vm, vm],
        out_specs=pl.BlockSpec(memory_space=pltpu.HBM),
        scratch_shapes=[
            pltpu.VMEM((width, width), f32),
            pltpu.VMEM((mine.size // LANES * 2, LANES), f32),
            pltpu.VMEM((3, width, width), jnp.bfloat16),
            pltpu.VMEM((rank, width), f32),
            pltpu.VMEM((rank, width), f32),
            pltpu.VMEM((rank, rank), f32),
            pltpu.SemaphoreType.DMA((3,)),
        ],
        compiler_params=pltpu.CompilerParams(vmem_limit_bytes=48 * 2**20),
        name="truncate",
    )(core, mine, other, start)


def counted(shape, axis):
    return lax.broadcasted_iota(jnp.int32, shape, axis)


def spread(levels, hours, places, turned=False):
    if turned:
        place, level = counted((places, 1), 0), counted((1, levels), 1)
    else:
        place, level = counted((1, places), 1), counted((levels, 1), 0)
    first = level * hours
    return jnp.where((place >= first) & (place < first + hours), 1.0, 0.0).astype(jnp.bfloat16)


def same(rows, columns, of):
    return of(counted((rows, 1), 0)) == of(counted((1, columns), 1))


def level_gram_kernel(scale, core_ref, field_ref, start_ref, mine_ref, other_ref, flat_ref, acc_ref, field_vmem, flat_vmem, sems, flat_sems):
    levels, hours, columns = field_ref.shape
    total = flat_ref.shape[0]
    chunk = columns // sems.shape[0]
    tile = 256
    copies, writes = [], []
    for c in range(sems.shape[0]):
        at = pl.ds(c * chunk, chunk)
        copies.append(pltpu.make_async_copy(field_ref.at[:, :, at], field_vmem.at[:, :, at], sems.at[c]))
        copies[c].start()
    for c, copy in enumerate(copies):
        copy.wait()
        flat = field_vmem[:, :, c * chunk : (c + 1) * chunk].reshape(levels * hours, chunk)
        flat = jnp.concatenate([flat, jnp.zeros((total - levels * hours, chunk), jnp.bfloat16)], axis=0)
        at = pl.ds(c * chunk, chunk)
        flat_vmem[:, at] = flat
        writes.append(pltpu.make_async_copy(flat_vmem.at[:, at], flat_ref.at[:, at], flat_sems.at[c]))
        writes[c].start()
        for j in range(0, total, tile):
            wide = min(tile, total - j)
            block = dot(flat[j:], flat[j : j + wide], ((1,), (1,)), None)
            acc_ref[j:, j : j + wide] = block if c == 0 else acc_ref[j:, j : j + wide] + block
    left = spread(levels, hours, total)
    right = spread(levels, hours, total, True)
    over = []
    for j in range(0, total, tile):
        wide = min(tile, total - j)
        row, col = counted((total - j, 1), 0), counted((1, wide), 1)
        weight = jnp.where(lax.rem(row, hours) == lax.rem(col, hours), jnp.where(row < wide, 0.5, 1.0), 0.0)
        half = acc_ref[j:, j : j + wide] * weight
        over.append(sum(dot(left[:, j:], part, precision=None) for part in reversed(split(half))))
    over = jnp.concatenate(over, axis=1)
    gram = sum(dot(part, right, precision=None) for part in reversed(split(over)))
    z = (dot(start_ref[...], gram) + dot(start_ref[...], gram, ((1,), (1,)))) * scale
    part = z.shape[0] // 2
    first = core_ref[0] == 0
    mine_ref[...] = jnp.where(first, z[:part], z[part:])
    other_ref[...] = jnp.where(first, z[part:], z[:part])
    for write in writes:
        write.wait()


def level_product(core, field, start, scale):
    levels, hours, columns = field.shape
    nmodes = start.shape[0]
    total = -(-levels * hours // 16) * 16
    smem, vm = pl.BlockSpec(memory_space=pltpu.SMEM), pl.BlockSpec(memory_space=pltpu.VMEM)
    return pl.pallas_call(
        functools.partial(level_gram_kernel, scale),
        out_shape=(
            jax.ShapeDtypeStruct((nmodes // 2, levels), jnp.float32),
            jax.ShapeDtypeStruct((nmodes // 2, levels), jnp.float32),
            jax.ShapeDtypeStruct((total, columns), jnp.bfloat16),
        ),
        in_specs=[smem, pl.BlockSpec(memory_space=pltpu.HBM), vm],
        out_specs=(vm, vm, pl.BlockSpec(memory_space=pltpu.HBM)),
        scratch_shapes=[
            pltpu.VMEM((total, total), jnp.float32),
            pltpu.VMEM((levels, hours, columns), jnp.bfloat16),
            pltpu.VMEM((total, columns), jnp.bfloat16),
            pltpu.SemaphoreType.DMA((4,)),
            pltpu.SemaphoreType.DMA((4,)),
        ],
        compiler_params=pltpu.CompilerParams(vmem_limit_bytes=58 * 2**20),
        name="level_product",
    )(core, field, start)


def project_kernel(hours, core_ref, mine_ref, other_ref, flat_ref, basis_ref, out_ref, weight_ref, linv_ref, z_ref, flat_vmem, sems):
    total, columns = flat_ref.shape
    chunk = columns // sems.shape[0]
    copies = []
    for c in range(sems.shape[0]):
        at = pl.ds(c * chunk, chunk)
        copies.append(pltpu.make_async_copy(flat_ref.at[:, at], flat_vmem.at[:, at], sems.at[c]))
        copies[c].start()
    nmodes, levels = z_ref.shape
    f32, bf16 = jnp.float32, jnp.bfloat16

    part = nmodes // 2
    z_ref[pl.ds(pl.multiple_of(part * core_ref[0], 8), part), :] = mine_ref[...]
    z_ref[pl.ds(pl.multiple_of(part * (1 - core_ref[0]), 8), part), :] = other_ref[...]
    z = z_ref[...]
    gram = dot(z, z, ((1,), (1,)))
    padded = jnp.concatenate([gram, jnp.zeros((nmodes, LANES - nmodes), f32)], axis=1)
    inverse_cholesky(padded, linv_ref)
    basis = dot(linv_ref[:, :nmodes], z)
    basis_ref[...] = basis
    modes_by_hours = spread(nmodes, hours, nmodes * hours, True)
    tall = dot(modes_by_hours, basis.astype(bf16), precision=None).astype(bf16)
    wide = dot(tall, spread(levels, hours, total), precision=None)
    weight_ref[...] = jnp.where(same(*wide.shape, lambda i: lax.rem(i, hours)), wide, 0.0).astype(bf16)

    groups, _, rows, _ = out_ref.shape
    for c, copy in enumerate(copies):
        copy.wait()
        made = dot(weight_ref[...], flat_vmem[:, c * chunk : (c + 1) * chunk], precision=None)
        for a in range(groups):
            for b in range(chunk // LANES):
                out_ref[a, c * chunk // LANES + b] = made[rows * a : rows * (a + 1), LANES * b : LANES * (b + 1)].astype(bf16)


def project(core, mine, other, flat, hours, groups):
    total, columns = flat.shape
    part, levels = mine.shape
    nmodes = 2 * part
    rows = hours * nmodes // groups
    smem, vm = pl.BlockSpec(memory_space=pltpu.SMEM), pl.BlockSpec(memory_space=pltpu.VMEM)
    return pl.pallas_call(
        functools.partial(project_kernel, hours),
        out_shape=(
            jax.ShapeDtypeStruct((nmodes, levels), jnp.float32),
            jax.ShapeDtypeStruct((groups, columns // LANES, rows, LANES), jnp.bfloat16),
        ),
        in_specs=[smem, vm, vm, pl.BlockSpec(memory_space=pltpu.HBM)],
        out_specs=(vm, vm),
        scratch_shapes=[
            pltpu.VMEM((hours * nmodes, total), jnp.bfloat16),
            pltpu.VMEM((nmodes, LANES), jnp.float32),
            pltpu.VMEM((nmodes, levels), jnp.float32),
            pltpu.VMEM((total, columns), jnp.bfloat16),
            pltpu.SemaphoreType.DMA((4,)),
        ],
        compiler_params=pltpu.CompilerParams(vmem_limit_bytes=53 * 2**20),
        name="project",
    )(core, mine, other, flat)


def upper(blocks):
    return [(i, j) for i in range(blocks) for j in range(i, blocks)]


def piece_rows(blocks):
    return -(-len(upper(blocks)) * LANES // (32 * 8)) * 8


def hour_gram_kernel(scale, blocks, core_ref, lag_ref, got_ref, out_ref, flat_ref, gram_ref, half_ref):
    senders, rows, _ = got_ref.shape
    f32, bf16 = jnp.float32, jnp.bfloat16
    hours = flat_ref.shape[0] // senders
    per = rows // hours
    many = 32
    size = many * rows
    new = counted((size, 1), 0)
    span = many * hours
    mode, rest = lax.div(new, span), lax.rem(new, span)
    wanted = lax.div(rest, hours) * rows + mode * hours + lax.rem(rest, hours)
    pick = jnp.where(counted((1, size), 1) == wanted, 1.0, 0.0).astype(bf16)
    for s in range(0, senders, 2 * many):
        pair = [got_ref[s + many * k : s + many * (k + 1)].reshape(size, LANES) for k in range(2)]
        moved = dot(pick, jnp.concatenate(pair, axis=1), precision=None).astype(bf16)
        for k in range(2):
            for m in range(per):
                flat_ref[hours * s + span * k : hours * s + span * (k + 1), LANES * m : LANES * (m + 1)] = moved[
                    span * m : span * (m + 1), LANES * k : LANES * (k + 1)
                ]
    for i in range(0, flat_ref.shape[0], 256):
        first = max(i - LANES, 0)
        band = dot(flat_ref[i : i + 256, :], flat_ref[first:, :], ((1,), (1,)), None)
        for b in range(first // LANES, gram_ref.shape[0]):
            gram_ref[b, i : i + 256, :] = band[:, LANES * b - first : LANES * (b + 1) - first]

    some = 16
    lane = lax.broadcasted_iota(jnp.int32, (some, LANES), 1)
    lags = [lag_ref[j] for j in range(lag_ref.shape[0])]
    whole = [lax.div(offset, LANES) for offset in lags]
    part = [lax.rem(offset, LANES) for offset in lags]
    spots = {pair: spot for spot, pair in enumerate(upper(blocks))}
    for i in range(blocks):
        for r in range(0, LANES, some):
            acc = {b: jnp.zeros((some, LANES), f32) for b in range(i, blocks)}
            for j, offset in enumerate(lags):
                load = {}
                for b in range(i, blocks + 1):
                    column = jnp.minimum(whole[j] + b, gram_ref.shape[0] - 1)
                    block = gram_ref[column, pl.ds(offset + LANES * i + r, some), :]
                    load[b] = pltpu.roll(block, lax.rem(LANES - part[j], LANES), 1)
                acc = {b: acc[b] + jnp.where(lane < LANES - part[j], load[b], load[b + 1]) for b in acc}
            for b in acc:
                at = LANES * spots[i, b] + r
                half_ref[at : at + some, :] = acc[b] * scale
    made = LANES * len(spots)
    half_ref[made:, :] = jnp.zeros((half_ref.shape[0] - made, LANES), f32)
    _, each, high, _ = out_ref.shape
    for c in range(2):
        for k in range(each):
            at = (c * each + k) * high
            out_ref[lax.bitwise_xor(c, core_ref[0]), k] = half_ref[at : at + high, :]


def hour_gram(core, lags, got, width, hours, scale):
    senders, rows, _ = got.shape
    total = senders * hours
    blocks = width // LANES
    high = piece_rows(blocks)
    smem, vm = pl.BlockSpec(memory_space=pltpu.SMEM), pl.BlockSpec(memory_space=pltpu.VMEM)
    return pl.pallas_call(
        functools.partial(hour_gram_kernel, scale, blocks),
        out_shape=jax.ShapeDtypeStruct((2, 16, high, LANES), jnp.float32),
        in_specs=[smem, smem, vm],
        out_specs=vm,
        scratch_shapes=[
            pltpu.VMEM((total, rows // hours * LANES), jnp.bfloat16),
            pltpu.VMEM((total // LANES, total, LANES), jnp.float32),
            pltpu.VMEM((32 * high, LANES), jnp.float32),
        ],
        compiler_params=pltpu.CompilerParams(vmem_limit_bytes=48 * 2**20),
        name="hour_gram",
    )(core, lags, got)


PLANE = ("y", "x")
COLUMN = ("zl", "zh")


def other_core(x):
    return lax.ppermute(x, "co", [(0, 1), (1, 0)])


def exchange(x, axes):
    return lax.all_to_all(x, axes, split_axis=0, concat_axis=0, tiled=True)


def collect(x, axes):
    return exchange(jnp.broadcast_to(x, (lax.axis_size(axes),) + x.shape), axes)


def sum_over(x, axes):
    return jnp.sum(collect(x, axes), axis=0)


def sum_pieces(pieces):
    here = pieces[0] + other_core(pieces[1])
    mine = jnp.sum(exchange(here, PLANE), axis=0)
    return collect(sum_over(mine, COLUMN), PLANE)


def body(field, level_start, time_start, lag_offsets):
    hour_count, levels, columns = field.shape
    devices = lax.axis_size(AXES)
    hours_all = hour_count * devices
    width = time_start.shape[0]
    nmodes = level_start.shape[1]
    core = lax.axis_index("co").reshape(1)
    scale = 1.0 / (hours_all * columns)
    z, other, level_hours = level_product(core, jnp.transpose(field, (1, 0, 2)), level_start.T, scale)
    z = z + other_core(other)
    z = sum_over(sum_over(z, PLANE), COLUMN)
    level_basis, sent = project(core, z, other_core(z), level_hours, hour_count, 8)
    sent = sent.reshape(devices, 24, LANES)
    received = exchange(sent, AXES)
    scale = 1.0 / (lag_offsets.shape[0] * nmodes * columns)
    summed = sum_pieces(hour_gram(core, lag_offsets, received, width, hour_count, scale))
    low_rank = truncate(core, summed, other_core(summed), time_start)
    return (level_basis.T, low_rank)


def solution(mesh):
    fine = Mesh(mesh.devices.reshape(SIZES), AXES)
    return jax.shard_map(
        body,
        mesh=fine,
        in_specs=(P(AXES, None, None), P(), P(), P()),
        out_specs=(P(), P()),
        check_vma=False,
    )
```
